512 devices in a mesh: lon: 64 (over y, z_lo, core), lat: 8 (over z_hi, x).
Axes of the slice: x: 4, y: 4, z: 16 (z_hi: 2, z_lo: 8; z = z_hi * 8 + z_lo), core: 2. Of those that a mesh axis runs over, the one named last changes fastest.
Arguments:
- features: bfloat16 [2, 192, 768, 512], P(None, 'lat', 'lon'), may hold values from -6 to 6
- region_ids: int32 [2, 192, 768], P(None, 'lat', 'lon'), may hold values from 0 to 2
- ln_gain: float32 [512], replicated, may hold values from 0.1 to 1.9
- ln_bias: float32 [512], replicated, may hold values from -3 to 3
- w_qkv: bfloat16 [512, 1536], replicated
- b_qkv: float32 [1536], replicated, may hold values from -2 to 2
- w_out: bfloat16 [512, 512], replicated, may hold values from -0.25 to 0.25
- b_out: float32 [512], replicated, may hold values from -2 to 2
Outputs:
- mixed: bfloat16 [2, 192, 768, 512], P(None, 'lat', 'lon')
The draws below stay inside these ranges and needn't reach their ends.
All inputs are finite; a program needn't handle non-finite values.
Results may differ from the reference program's by a relative error of at most 0.0056.
Values may be sent and summed in bfloat16 or wider, within the bound.
No kernel may reach another device: no remote copies, remote signals or barrier semaphores. Data moves between devices by JAX's collectives and lax.ppermute only.
A program may use at most 128 MiB of HBM per device.

```python
import jax
import jax.numpy as jnp
from jax import lax

D = 512
HEADS = 8
LEV = 2
WLAT = 6
WLON = 12
SLAT = 3
SLON = 6
NLAT = 192
NLON = 768


def draw_w_qkv(key, part):
    key = jax.random.fold_in(key, 11)
    first = jax.random.fold_in(key, 0)
    base = jax.random.normal(first, (D, 3 * D), jnp.float32) * D ** (-0.5)
    return base.astype(jnp.bfloat16)


def with_ends(values, own_key, low, high):
    dims = values.shape
    place = [jax.random.randint(jax.random.fold_in(own_key, axis), (), 0, dims[axis]) for axis in range(len(dims))]
    values = values.at[tuple(place)].set(low)
    longest = dims.index(max(dims))
    place[longest] = (place[longest] + 1) % dims[longest]
    return values.at[tuple(place)].set(high)


def block_scale(key, shape, pieces, smallest, top_value):
    level, own = 1.0, jax.random.fold_in(key, 6)
    for position, parts in pieces:
        draws = jnp.exp(jax.random.uniform(jax.random.fold_in(own, position), (parts,), jnp.float32, smallest / len(pieces), top_value / len(pieces)))
        level = level * jnp.repeat(draws, shape[position] // parts).reshape([-1 if axis == position else 1 for axis in range(len(shape))])
    return level


def gaussian(rng, dims, scale, limit, cuts=(), dtype=jnp.bfloat16):
    factor_of = block_scale(rng, dims, cuts, -0.22, 0.18) if cuts else 1.0
    values = jax.random.normal(rng, dims, jnp.float32) * scale * factor_of
    return jnp.minimum(jnp.maximum(values, -limit), limit).astype(dtype)


def setup_inputs(seed: int = 0) -> dict:
    key_list = jax.random.split(jax.random.key(seed), 9)
    features = gaussian(key_list[0], (LEV, NLAT, NLON, D), 1.0, 6.0, ((1, 8), (2, 64)))
    region_ids = with_ends(jax.random.randint(key_list[1], (LEV, NLAT, NLON), 0, 3), jax.random.fold_in(key_list[1], 1), 0, 2).astype(jnp.int32)
    ln_gain = jnp.clip(1.0 + 0.18 * jax.random.normal(key_list[2], (D,), jnp.float32), 0.1, 1.9)
    ln_bias = gaussian(key_list[3], (D,), 0.5, 3.0, (), jnp.float32)
    w_qkv = draw_w_qkv(jax.random.fold_in(key_list[8], 71), 0)
    b_qkv = gaussian(key_list[5], (3 * D,), 0.3, 2.0, (), jnp.float32)
    w_out = gaussian(key_list[6], (D, D), D ** -0.5, 0.25)
    b_out = gaussian(key_list[7], (D,), 0.3, 2.0, (), jnp.float32)
    return dict(features=features, region_ids=region_ids, ln_gain=ln_gain, ln_bias=ln_bias, w_qkv=w_qkv, b_qkv=b_qkv, w_out=w_out, b_out=b_out)


def to_windows(array, rows, cols):
    levels = array.shape[0]
    last = array.shape[-1]
    shaped = array.reshape(levels, rows // WLAT, WLAT, cols // WLON, WLON, last)
    return shaped.transpose(1, 3, 0, 2, 4, 5).reshape(-1, levels * WLAT * WLON, last)

def from_windows(array, levels, rows, cols):
    last = array.shape[-1]
    shaped = array.reshape(rows // WLAT, cols // WLON, levels, WLAT, WLON, last)
    return shaped.transpose(2, 0, 3, 1, 4, 5).reshape(levels, rows, cols, last)

def attend(tile, labels, ln_gain, ln_bias, w_qkv, b_qkv, w_out, b_out):
    levels, rows, cols, width = tile.shape
    values = tile.astype(jnp.float32)
    center = values - lax.optimization_barrier(jnp.mean(values, axis=-1, keepdims=True))
    spread = lax.optimization_barrier(jnp.mean(center * center, axis=-1, keepdims=True))
    normed = (center * lax.rsqrt(spread + 1e-05) * ln_gain + ln_bias).astype(jnp.bfloat16)
    windows = to_windows(normed, rows, cols)
    marks = to_windows(labels[..., None], rows, cols)[..., 0]
    count, span = (windows.shape[0], windows.shape[1])
    head_size = width // HEADS
    packed = jnp.dot(windows.reshape(count * span, width), w_qkv, preferred_element_type=jnp.float32) + b_qkv
    packed = packed.astype(jnp.bfloat16).reshape(count, span, 3, HEADS, head_size)
    query = packed[:, :, 0].astype(jnp.float32)
    keys = packed[:, :, 1].astype(jnp.float32)
    vals = packed[:, :, 2].astype(jnp.float32)
    scores = jnp.einsum('nqhd,nkhd->nhqk', query, keys) * head_size ** (-0.5)
    allowed = marks[:, None, :, None] == marks[:, None, None, :]
    scores = jnp.where(allowed, scores, -1e+30)
    top = lax.optimization_barrier(jnp.max(scores, axis=-1, keepdims=True))
    expd = jnp.exp(scores - top)
    weights = (expd / lax.optimization_barrier(jnp.sum(expd, axis=-1, keepdims=True))).astype(jnp.bfloat16)
    heads_out = jnp.einsum('nhqk,nkhd->nqhd', weights.astype(jnp.float32), vals)
    heads_out = heads_out.astype(jnp.bfloat16).reshape(count * span, width)
    projected = (jnp.dot(heads_out, w_out, preferred_element_type=jnp.float32) + b_out).astype(jnp.bfloat16)
    return from_windows(projected.reshape(count, span, width), levels, rows, cols)

def reference(features, region_ids, ln_gain, ln_bias, w_qkv, b_qkv, w_out, b_out):
    shifted = jnp.roll(features, (-SLAT, -SLON), axis=(1, 2))
    shifted_ids = jnp.roll(region_ids, (-SLAT, -SLON), axis=(1, 2))
    flags = (jnp.arange(NLAT) + SLAT) % NLAT < SLAT
    labels = shifted_ids.astype(jnp.float32) + 4.0 * flags.astype(jnp.float32)[None, :, None]
    blocks = NLAT // WLAT
    tiles = shifted.reshape(LEV, blocks, WLAT, NLON, D).transpose(1, 0, 2, 3, 4)
    label_tiles = labels.reshape(LEV, blocks, WLAT, NLON).transpose(1, 0, 2, 3)

    def one_block(pair):
        return attend(pair[0], pair[1], ln_gain, ln_bias, w_qkv, b_qkv, w_out, b_out)
    result = lax.map(one_block, (tiles, label_tiles))
    result = result.transpose(1, 0, 2, 3, 4).reshape(LEV, NLAT, NLON, D)
    attended = jnp.roll(result, (SLAT, SLON), axis=(1, 2))
    return (features.astype(jnp.float32) + attended.astype(jnp.float32)).astype(jnp.bfloat16)
```

```python
import jax
import jax.numpy as jnp
from jax import lax
from jax.experimental import pallas as pl
from jax.experimental.pallas import tpu as pltpu
from jax.sharding import PartitionSpec as P

HEADS = 8
WLAT = 6
WLON = 12
SLAT = 3
SLON = 6
LEV = 2
D = 512
HS = D // HEADS
ROWS = 24
COLS = 12
HALF = WLAT * LEV * SLON
BLOCKS = ROWS // WLAT
SIDE = BLOCKS * HALF
PAY = SIDE + 16
STRIP = 16
BLK = WLAT * LEV * STRIP
EDGE = 40
KPAY = 4 * EDGE + 16
F32 = jnp.float32
BF16 = jnp.bfloat16
LIMIT = 60 * 1024 * 1024


def mm(a, b):
    return jnp.dot(a, b, preferred_element_type=F32)


def mm_nt(a, b):
    return lax.dot_general(a, b, (((1,), (1,)), ((), ())), preferred_element_type=F32)


def iota(shape, dim):
    return lax.broadcasted_iota(jnp.int32, shape, dim)


def place_of(k, odd_lon):
    strip, c16 = k >> 4, k & 15
    half = jnp.where(c16 >= SLON, 1, 0)
    side = half + odd_lon - 2 * half * odd_lon
    t = side * HALF + (strip >> 1) * 12 + (strip & 1) * 6 + (c16 - SLON * half)
    return jnp.where(c16 < COLS, t, -1)


def layer_norm(x, gain, bias):
    center = x - jnp.mean(x, axis=-1, keepdims=True)
    spread = jnp.mean(center * center, axis=-1, keepdims=True)
    return (center * lax.rsqrt(spread + 1e-05) * gain + bias).astype(BF16)


def edge_rows():
    odd = lax.axis_index("lat") % 2
    return (ROWS - SLAT) * odd, (ROWS - SLAT) * (1 - odd)


def prep_kernel(feat, ids, pay1, pay2, qlab, x_scr, b_scr, lab_scr):
    odd_lon = lax.axis_index("lon") % 2
    first = lax.axis_index("lat") == 0
    e1, e2 = edge_rows()
    x_scr[...] = jnp.zeros_like(x_scr)
    for i in range(ROWS):
        for l in range(LEV):
            x_scr[(i * LEV + l) * STRIP : (i * LEV + l) * STRIP + COLS, :] = feat[l, i]
    lab_scr[...] = jnp.zeros_like(lab_scr)
    from_first = jnp.where((iota((ROWS, COLS), 0) < SLAT) & first, 4.0, 0.0)
    for l in range(LEV):
        lab_scr[l * ROWS : (l + 1) * ROWS, :COLS] = ids[l].astype(F32) + from_first
    n = ROWS * LEV * STRIP
    strip = iota((n, ROWS * LEV), 0) >> 4
    pick = ((strip & 1) * ROWS + (strip >> 1)) == iota((n, ROWS * LEV), 1)
    spread = mm(jnp.where(pick, 1.0, 0.0).astype(BF16), lab_scr[...].astype(BF16))
    b_scr[...] = jnp.where((iota((n, 128), 0) & 15) == iota((n, 128), 1), spread, 0.0).astype(BF16)

    order = (iota((2 * HALF, BLK), 0) == place_of(iota((2 * HALF, BLK), 1), odd_lon))
    order = jnp.where(order, 1.0, 0.0).astype(BF16)

    def block(ref, b):
        if b < BLOCKS - 1:
            at = (SLAT + WLAT * b) * LEV * STRIP
            return ref[at : at + BLK, :]
        parts = [ref[pl.ds(pl.multiple_of(e * LEV * STRIP, 32), BLK // 2), :] for e in (e1, e2)]
        return jnp.concatenate(parts, axis=0)

    tokens = [mm(order, block(x_scr, b)) for b in range(BLOCKS)]
    marks = [mm(order, block(b_scr, b)) for b in range(BLOCKS)]
    for s, pay in enumerate((pay1, pay2)):
        own = slice(s * HALF, (s + 1) * HALF)
        pay[:SIDE, :] = jnp.concatenate([t[own] for t in tokens], axis=0).astype(BF16)
        mark = jnp.concatenate([m[own] for m in marks], axis=0)
        qlab[s] = jnp.broadcast_to(jnp.sum(mark, axis=-1, keepdims=True), (SIDE, 128))
        line = mm_nt(jnp.ones((STRIP, 128), BF16), mark.astype(BF16))
        pay[SIDE:, :] = jnp.concatenate(
            [line, jnp.zeros((STRIP, D - SIDE), F32)], axis=1
        ).astype(BF16)


def own_kernel(pay1, pay2, gain, bias, w_qkv, b_qkv, qkv):
    g, b = gain[...].reshape(1, D), bias[...].reshape(1, D)
    for s, pay in enumerate((pay1, pay2)):
        normed = layer_norm(pay[:SIDE, :].astype(F32), g, b)
        for c in range(3):
            cols = slice(c * D, (c + 1) * D)
            part = mm(normed, w_qkv[:, cols]) + b_qkv[cols].reshape(1, D)
            part = part.astype(BF16).astype(F32)
            if c == 0:
                part = part * HS ** (-0.5)
            for m in range(BLOCKS):
                qkv[s, m, :, cols] = part[m * HALF : (m + 1) * HALF].astype(BF16)


def label_line(ref, at):
    return ref[at : at + STRIP, :].astype(F32)[:8]


def shifted(line, start, to, wide):
    return pltpu.roll(line, (to - start) % D, 1)[:1, :wide]


def attention(q, k, v, q_label, k_label):
    n = q.shape[0]
    keys = k.shape[0]
    wide = 4 * HS
    allowed = q_label == k_label
    out = []
    col = iota((1, wide), 1)
    for g in range(2):
        cols = slice(g * wide, (g + 1) * wide)
        own = [(col >= h * HS) & (col < (h + 1) * HS) for h in range(4)]
        qg = q[:, cols]
        stacked = jnp.concatenate([jnp.where(o, qg, 0.0) for o in own], axis=0).astype(BF16)
        scores = mm_nt(stacked, k[:, cols])
        scores = jnp.where(allowed[None], scores.reshape(4, n, keys), -1e30)
        top = jnp.max(scores, axis=-1, keepdims=True)
        expd = jnp.exp(scores - top)
        weights = (expd / jnp.sum(expd, axis=-1, keepdims=True)).astype(BF16)
        full = mm(weights.reshape(4 * n, keys), v[:, cols])
        picked = jnp.where(own[0], full[:n], 0.0)
        for h in range(1, 4):
            picked = jnp.where(own[h], full[h * n : (h + 1) * n], picked)
        out.append(picked)
    return jnp.concatenate(out, axis=1)


def finish(heads, x, w_out, b_out, back):
    projected = (mm(heads.astype(BF16), w_out) + b_out).astype(BF16).astype(F32)
    return mm(back, (x + projected).astype(BF16)).astype(BF16)


def order_back():
    odd_lon = lax.axis_index("lon") % 2
    back = iota((BLK, 2 * HALF), 1) == place_of(iota((BLK, 2 * HALF), 0), odd_lon)
    return jnp.where(back, 1.0, 0.0).astype(BF16)


def edges_kernel(pay1, pay2, far1, far2, out1, out2):
    lane = iota((8, D), 1)
    for e, out in enumerate((out1, out2)):
        at = 32 * e
        rows, line = [], jnp.zeros((8, D), F32)
        for j, ref in enumerate((pay1, far1, pay2, far2)):
            rows.append(ref[SIDE - 80 : SIDE, :].astype(F32)[8 + at : 8 + at + EDGE])
            moved = pltpu.roll(label_line(ref, SIDE), (j * EDGE - (3 * HALF + at)) % D, 1)
            line = jnp.where((lane >= j * EDGE) & (lane < (j + 1) * EDGE), moved, line)
        out[: 4 * EDGE, :] = jnp.concatenate(rows, axis=0).astype(BF16)
        out[4 * EDGE :, :] = jnp.concatenate([line, line], axis=0).astype(BF16)


def inner_kernel(pay1, pay2, far1, far2, qlab, qkv, gain, bias, w_qkv, b_qkv, w_out, b_out, kv_edge, out, kv, done, sem):
    g, b = gain[...].reshape(1, D), bias[...].reshape(1, D)
    for s, far in enumerate((far1, far2)):
        normed = layer_norm(far[:SIDE, :].astype(F32), g, b)
        for c in range(2):
            cols = slice((c + 1) * D, (c + 2) * D)
            part = mm(normed, w_qkv[:, cols]) + b_qkv[cols].reshape(1, D)
            kv[s, :, c * D : (c + 1) * D] = part
            kv_edge[s, :, c * D : (c + 1) * D] = part[3 * HALF :].astype(BF16)
    back = order_back()
    for m in range(BLOCKS - 1):
        rows = slice(m * HALF, (m + 1) * HALF)
        heads, xs = [], []
        for s, (pay, far) in enumerate(((pay1, far1), (pay2, far2))):
            both = jnp.concatenate([qkv[s, m, :, D:].astype(F32), kv[s, rows, :]], axis=0).astype(BF16)
            own_line = shifted(label_line(pay, SIDE), m * HALF, 0, 2 * HALF)
            far_line = shifted(label_line(far, SIDE), m * HALF, HALF, 2 * HALF)
            k_label = jnp.where(iota((1, 2 * HALF), 1) < HALF, own_line, far_line)
            q_label = qlab[s, rows, :][:, :1]
            heads.append(attention(qkv[s, m, :, :D].astype(F32), both[:, :D], both[:, D:], q_label, k_label))
            xs.append(pay[:SIDE, :].astype(F32)[rows])
        strips = finish(
            jnp.concatenate(heads, axis=0), jnp.concatenate(xs, axis=0), w_out[...], b_out[...].reshape(1, D), back
        )
        for r in range(WLAT):
            for l in range(LEV):
                at = (r * LEV + l) * STRIP
                done[l, m * WLAT + r] = strips[at : at + COLS]
    copy = pltpu.make_async_copy(done, out.at[:, SLAT : ROWS - SLAT], sem)
    copy.start()
    copy.wait()


def outer_kernel(pay1, pay2, far1, far2, over1, over2, qlab, qkv, kv_edge, gain, bias, w_qkv, b_qkv, w_out, b_out, so_far, out, done1, done2, sem):
    del so_far
    g, b = gain[...].reshape(1, D), bias[...].reshape(1, D)
    e1, e2 = edge_rows()
    last = BLOCKS - 1
    results = []
    for e, over in enumerate((over1, over2)):
        normed = layer_norm(over[: 4 * EDGE, :].astype(F32), g, b)
        kv = [
            mm(normed, w_qkv[:, (c + 1) * D : (c + 2) * D]) + b_qkv[(c + 1) * D : (c + 2) * D].reshape(1, D)
            for c in range(2)
        ]
        for s, (pay, far) in enumerate(((pay1, far1), (pay2, far2))):
            keys = []
            for c in range(2):
                cols = slice(c * D, (c + 1) * D)
                own = qkv[s, last, :, (c + 1) * D : (c + 2) * D].astype(F32)
                keys.append(
                    jnp.concatenate(
                        [own, kv_edge[s, :, cols].astype(F32), kv[c][2 * EDGE * s : 2 * EDGE * (s + 1)]], axis=0
                    ).astype(BF16)
                )
            count = 2 * HALF + 2 * EDGE
            lane = iota((1, count), 1)
            own_line = shifted(label_line(pay, SIDE), last * HALF, 0, count)
            far_line = shifted(label_line(far, SIDE), last * HALF, HALF, count)
            over_line = shifted(label_line(over, 4 * EDGE), 2 * EDGE * s, 2 * HALF, count)
            k_label = jnp.where(lane < HALF, own_line, jnp.where(lane < 2 * HALF, far_line, over_line))
            piece = lane - 2 * HALF
            piece = jnp.where(piece >= EDGE, piece - EDGE, piece)
            spot = jnp.where(lane < HALF, lane, jnp.where(lane < 2 * HALF, lane - HALF, piece))
            if e == 0:
                mine = spot < HALF // 2
            else:
                mine = spot >= jnp.where(lane < 2 * HALF, HALF // 2, EDGE - HALF // 2)
            k_label = jnp.where(mine, k_label, -1.0)
            at = 32 * e
            q = qkv[s, last, :, :D].astype(F32)[at : at + EDGE]
            q_label = qlab[s, last * HALF : SIDE, :][at : at + EDGE, :1]
            results.append(attention(q, keys[0], keys[1], q_label, k_label))
    heads, xs = [], []
    for s, pay in enumerate((pay1, pay2)):
        a, z = results[s], results[2 + s]
        mid = jnp.where(iota((8, 1), 0) < 4, a[32:], z[:8])
        heads.append(jnp.concatenate([a[:32], mid, z[8:]], axis=0))
        xs.append(pay[:SIDE, :].astype(F32)[last * HALF :])
    strips = finish(
        jnp.concatenate(heads, axis=0),
        jnp.concatenate(xs, axis=0),
        w_out[...],
        b_out[...].reshape(1, D),
        order_back(),
    )
    for r in range(WLAT):
        for l in range(LEV):
            at = (r * LEV + l) * STRIP
            (done1 if r < SLAT else done2)[l, r % SLAT] = strips[at : at + COLS]
    copies = [
        pltpu.make_async_copy(done, out.at[:, pl.ds(e, SLAT)], sem.at[i])
        for i, (done, e) in enumerate(((done1, e1), (done2, e2)))
    ]
    for copy in copies:
        copy.start()
    for copy in copies:
        copy.wait()


VMEM = pl.BlockSpec(memory_space=pltpu.VMEM)
ANY = pl.BlockSpec(memory_space=pl.ANY)


def params(**more):
    return pltpu.CompilerParams(vmem_limit_bytes=LIMIT, **more)


def cost(flops, moved, exps=0):
    return pl.CostEstimate(flops=flops, bytes_accessed=moved, transcendentals=exps)


def swap(block, axis, first):
    n = lax.axis_size(axis)
    route = []
    for i in range(first, n, 2):
        route += [(i, (i + 1) % n), ((i + 1) % n, i)]
    return lax.ppermute(block, axis, route)


def local(features, region_ids, ln_gain, ln_bias, w_qkv, b_qkv, w_out, b_out):
    shape = jax.ShapeDtypeStruct
    pay1, pay2, qlab = pl.pallas_call(
        prep_kernel,
        out_shape=[shape((PAY, D), BF16), shape((PAY, D), BF16), shape((2, SIDE, 128), F32)],
        in_specs=[VMEM, VMEM],
        out_specs=[VMEM] * 3,
        scratch_shapes=[
            pltpu.VMEM((ROWS * LEV * STRIP, D), BF16),
            pltpu.VMEM((ROWS * LEV * STRIP, 128), BF16),
            pltpu.VMEM((ROWS * LEV, 128), F32),
        ],
        compiler_params=params(),
        cost_estimate=cost(4 * 144 * 192 * 640 * 2, 2_000_000),
        name="prep",
    )(features, region_ids)
    far1 = swap(pay1, "lon", 1)
    far2 = swap(pay2, "lon", 0)
    qkv = pl.pallas_call(
        own_kernel,
        out_shape=shape((2, BLOCKS, HALF, 3 * D), BF16),
        in_specs=[VMEM] * 6,
        out_specs=VMEM,
        compiler_params=params(),
        cost_estimate=cost(2 * SIDE * D * 3 * D * 2, 4_000_000),
        name="own",
    )(pay1, pay2, ln_gain, ln_bias, w_qkv, b_qkv)
    edge1, edge2 = pl.pallas_call(
        edges_kernel,
        out_shape=[shape((KPAY, D), BF16)] * 2,
        in_specs=[VMEM] * 4,
        out_specs=[VMEM] * 2,
        compiler_params=params(),
        cost_estimate=cost(1_000_000, 500_000),
        name="edges",
    )(pay1, pay2, far1, far2)
    over1 = swap(edge1, "lat", 1)
    over2 = swap(edge2, "lat", 0)
    kv_edge, so_far = pl.pallas_call(
        inner_kernel,
        out_shape=[shape((2, HALF, 2 * D), BF16), shape(features.shape, BF16)],
        in_specs=[VMEM] * 12,
        out_specs=[VMEM, ANY],
        scratch_shapes=[
            pltpu.VMEM((2, SIDE, 2 * D), F32),
            pltpu.VMEM((LEV, ROWS - 2 * SLAT, COLS, D), BF16),
            pltpu.SemaphoreType.DMA(()),
        ],
        compiler_params=params(),
        cost_estimate=cost(3_000_000_000, 5_000_000, 500_000),
        name="inner",
    )(pay1, pay2, far1, far2, qlab, qkv, ln_gain, ln_bias, w_qkv, b_qkv, w_out, b_out)
    return pl.pallas_call(
        outer_kernel,
        out_shape=shape(features.shape, BF16),
        in_specs=[VMEM] * 15 + [ANY],
        out_specs=ANY,
        scratch_shapes=[
            pltpu.VMEM((LEV, SLAT, COLS, D), BF16),
            pltpu.VMEM((LEV, SLAT, COLS, D), BF16),
            pltpu.SemaphoreType.DMA((2,)),
        ],
        input_output_aliases={15: 0},
        compiler_params=params(),
        cost_estimate=cost(1_500_000_000, 5_000_000, 200_000),
        name="outer",
    )(pay1, pay2, far1, far2, over1, over2, qlab, qkv, kv_edge, ln_gain, ln_bias, w_qkv, b_qkv, w_out, b_out, so_far)


def solution(mesh):
    return jax.shard_map(
        local,
        mesh=mesh,
        in_specs=(P(None, "lat", "lon", None), P(None, "lat", "lon"), P(), P(), P(), P(), P(), P()),
        out_specs=P(None, "lat", "lon", None),
        check_vma=False,
    )
```

```python
import functools

import jax
import jax.numpy as jnp
from jax import lax
from jax.experimental import pallas as pl
from jax.experimental.pallas import tpu as pltpu
from jax.sharding import PartitionSpec as P

HEADS = 8
WLAT = 6
WLON = 12
SLAT = 3
SLON = 6
LEV = 2
D = 512
HS = D // HEADS
ROWS = 24
COLS = 12
HALF = WLAT * LEV * SLON
BLOCKS = ROWS // WLAT
SIDE = BLOCKS * HALF
PAY = SIDE + 16
EDGE = 40
LAT_RUN = 4
LON_RUN = 16
F32 = jnp.float32
BF16 = jnp.bfloat16
LIMIT = 24 * 1024 * 1024


def mm(a, b):
    return jnp.dot(a, b, preferred_element_type=F32)


def mm_nt(a, b):
    return lax.dot_general(a, b, (((1,), (1,)), ((), ())), preferred_element_type=F32)


def iota(shape, dim):
    return lax.broadcasted_iota(jnp.int32, shape, dim)


def place_of(n, odd_lat):
    l = jnp.where(n >= SIDE // 2, 1, 0)
    n = n - SIDE // 2 * l
    c = sum(jnp.where(n >= ROWS * q, 1, 0) for q in range(1, SLON))
    i = n - ROWS * c
    top = 3 * HALF + HALF // 2 * odd_lat + 12 * i
    bottom = 3 * HALF + HALF // 2 * (1 - odd_lat) + 12 * (i - (ROWS - SLAT))
    base = jnp.where(i < SLAT, top, jnp.where(i >= ROWS - SLAT, bottom, 12 * (i - SLAT)))
    return base + SLON * l + c, i, LEV * c + l


def layer_norm(x, gain, bias):
    center = x - jnp.mean(x, axis=-1, keepdims=True)
    spread = jnp.mean(center * center, axis=-1, keepdims=True)
    return (center * lax.rsqrt(spread + 1e-05) * gain + bias).astype(BF16)


def side_rows(s, l):
    odd = lax.axis_index("lon") % 2
    half = odd if s == 0 else 1 - odd
    return pl.multiple_of(l * SIDE + half * (SIDE // 2), SIDE // 2)


def prep_kernel(feat, ids, pay1, pay2, qlab, lab):
    odd_lon = lax.axis_index("lon") % 2
    odd_lat = lax.axis_index("lat") % 2
    first = lax.axis_index("lat") == 0
    place, lat, strip = place_of(iota((1, SIDE), 1), odd_lat)
    order = jnp.where(iota((SIDE, SIDE), 0) == place, 1.0, 0.0)
    spread = jnp.where(iota((128, SIDE), 0) == lat, 1.0, 0.0).astype(BF16)
    from_first = jnp.where((iota((LEV, ROWS), 1) < SLAT) & first, 4.0, 0.0)
    lab[...] = jnp.zeros_like(lab)
    for s, pay in enumerate((pay1, pay2)):
        tokens = jnp.concatenate([feat[pl.ds(side_rows(s, l), SIDE // 2), :] for l in range(LEV)], axis=0)
        pay[:SIDE, :] = mm(order.astype(BF16), tokens).astype(BF16)
        half = odd_lon if s == 0 else 1 - odd_lon
        for c in range(SLON):
            lab[s, LEV * c : LEV * (c + 1), :ROWS] = ids[SLON * half + c].astype(F32) + from_first
        line = mm(lab[s].astype(BF16), spread)
        line = jnp.sum(jnp.where(iota((16, SIDE), 0) == strip, line, 0.0), axis=0, keepdims=True)
        qlab[s] = jnp.broadcast_to(jnp.sum(order * line, axis=-1, keepdims=True), (SIDE, 128))
        line = mm_nt(jnp.broadcast_to(line, (16, SIDE)).astype(BF16), order.astype(BF16))
        pay[SIDE:, :] = jnp.concatenate([line, jnp.zeros((16, D - SIDE), F32)], axis=1).astype(BF16)


def own_kernel(pay1, pay2, gain, bias, w_qkv, b_qkv, qkv):
    g, b = gain[...].reshape(1, D), bias[...].reshape(1, D)
    for s, pay in enumerate((pay1, pay2)):
        normed = layer_norm(pay[:SIDE, :].astype(F32), g, b)
        for c in range(3):
            cols = slice(c * D, (c + 1) * D)
            part = mm(normed, w_qkv[:, cols]) + b_qkv[cols].reshape(1, D)
            part = part.astype(BF16).astype(F32)
            if c == 0:
                part = part * HS ** (-0.5)
            for m in range(BLOCKS):
                qkv[s, m, :, cols] = part[m * HALF : (m + 1) * HALF].astype(BF16)


def label_line(ref, at):
    return ref[...].astype(F32)[at : at + 8]


def shifted(line, start, to):
    return pltpu.roll(line, (to - start) % D, 1)


def attention(q, k, v, q_label, k_label):
    n = q.shape[0]
    keys = k.shape[0]
    wide = 4 * HS
    allowed = q_label == k_label
    out = []
    col = iota((1, wide), 1)
    for g in range(2):
        cols = slice(g * wide, (g + 1) * wide)
        own = [(col >= h * HS) & (col < (h + 1) * HS) for h in range(4)]
        qg = q[:, cols]
        stacked = jnp.concatenate([jnp.where(o, qg, 0.0) for o in own], axis=0).astype(BF16)
        scores = mm_nt(stacked, k[:, cols])
        scores = jnp.where(allowed[None], scores.reshape(4, n, keys), -1e30)
        top = jnp.max(scores, axis=-1, keepdims=True)
        expd = jnp.exp(scores - top)
        weights = (expd / jnp.sum(expd, axis=-1, keepdims=True)).astype(BF16)
        full = mm(weights.reshape(4 * n, keys), v[:, cols])
        picked = jnp.where(own[0], full[:n], 0.0)
        for h in range(1, 4):
            picked = jnp.where(own[h], full[h * n : (h + 1) * n], picked)
        out.append(picked)
    return jnp.concatenate(out, axis=1)


def finish(heads, x, w_out, b_out):
    projected = (mm(heads.astype(BF16), w_out) + b_out).astype(BF16).astype(F32)
    return (x + projected).astype(BF16)


def edge_piece(ref, e):
    at = 3 * HALF + 32 * e
    return ref[...].astype(F32)[at : at + EDGE]


def edge_labels(parts):
    lane = iota((8, D), 1)
    out = jnp.zeros((8, D), F32)
    for j, (line, start) in enumerate(parts):
        out = jnp.where((lane >= j * EDGE) & (lane < (j + 1) * EDGE), shifted(line, start, j * EDGE), out)
    return out


def edge_kernel(e, *refs):
    sides, out = refs[:-1], refs[-1]
    rows = [edge_piece(ref, e) for ref in sides]
    line = edge_labels([(label_line(ref, SIDE), 3 * HALF + 32 * e) for ref in sides])
    rows += [line] * ((out.shape[0] - len(rows) * EDGE) // 8)
    out[...] = jnp.concatenate(rows, axis=0).astype(BF16)


def far_pairs(axis, size):
    at = lax.axis_index(axis)
    return (at % size == 0) | (at % size == size - 1)


def corner_kernel(pay1, far1, over1, out):
    lat_far = far_pairs("lat", LAT_RUN)
    both_far = lat_far & far_pairs("lon", LON_RUN)
    a, b, c = edge_piece(pay1, 0), edge_piece(far1, 0), over1[...].astype(F32)[:EDGE]
    la, lb = (shifted(label_line(ref, SIDE), 3 * HALF, 0) for ref in (pay1, far1))
    lc = label_line(over1, 3 * EDGE)
    one = jnp.where(both_far, 1.0, 0.0)
    two = jnp.where(lat_far, 1.0, 0.0)

    def choose(a, b, c):
        return jnp.where(jnp.full(a.shape, one) > 0.5, a, jnp.where(jnp.full(a.shape, two) > 0.5, c, b))

    out[...] = jnp.concatenate([choose(a, b, c), choose(la, lb, lc)], axis=0).astype(BF16)


def inner_kernel(pay1, pay2, far1, far2, qlab, qkv, gain, bias, w_qkv, b_qkv, w_out, b_out, kv_edge, mixed, back, kv):
    g, b = gain[...].reshape(1, D), bias[...].reshape(1, D)
    for s, far in enumerate((far1, far2)):
        normed = layer_norm(far[:SIDE, :].astype(F32), g, b)
        for c in range(2):
            cols = slice((c + 1) * D, (c + 2) * D)
            part = mm(normed, w_qkv[:, cols]) + b_qkv[cols].reshape(1, D)
            kv[s, :, c * D : (c + 1) * D] = part
            kv_edge[s, :, c * D : (c + 1) * D] = part[3 * HALF :].astype(BF16)
    place, _, _ = place_of(iota((SIDE, 1), 0), lax.axis_index("lat") % 2)
    back[...] = jnp.where(iota((SIDE, SIDE), 1) == place, 1.0, 0.0).astype(BF16)
    for m in range(BLOCKS - 1):
        rows = slice(m * HALF, (m + 1) * HALF)
        heads, xs = [], []
        for s, (pay, far) in enumerate(((pay1, far1), (pay2, far2))):
            both = jnp.concatenate([qkv[s, m, :, D:].astype(F32), kv[s, rows, :]], axis=0).astype(BF16)
            own_line = shifted(label_line(pay, SIDE), m * HALF, 0)[:1, : 2 * HALF]
            far_line = shifted(label_line(far, SIDE), m * HALF, HALF)[:1, : 2 * HALF]
            k_label = jnp.where(iota((1, 2 * HALF), 1) < HALF, own_line, far_line)
            q_label = qlab[s, rows, :][:, :1]
            heads.append(attention(qkv[s, m, :, :D].astype(F32), both[:, :D], both[:, D:], q_label, k_label))
            xs.append(pay[:SIDE, :].astype(F32)[rows])
        done = finish(jnp.concatenate(heads, axis=0), jnp.concatenate(xs, axis=0), w_out[...], b_out[...].reshape(1, D))
        mixed[0, m] = done[:HALF]
        mixed[1, m] = done[HALF:]


def project_kv(x, g, b, w_qkv, b_qkv):
    normed = layer_norm(x, g, b)
    return [
        mm(normed, w_qkv[:, (c + 1) * D : (c + 2) * D]) + b_qkv[(c + 1) * D : (c + 2) * D].reshape(1, D) for c in range(2)
    ]


def edge_window(e, s, pay, far, over_kv, over_line, qlab, qkv, kv_edge):
    last = BLOCKS - 1
    keys = []
    for c in range(2):
        own = qkv[s, last, :, (c + 1) * D : (c + 2) * D].astype(F32)
        far_part = kv_edge[s, :, c * D : (c + 1) * D].astype(F32)
        keys.append(jnp.concatenate([own, far_part, over_kv[c]], axis=0).astype(BF16))
    count = 2 * HALF + 2 * EDGE
    lane = iota((1, count), 1)
    own_line = shifted(label_line(pay, SIDE), last * HALF, 0)[:1, :count]
    far_line = shifted(label_line(far, SIDE), last * HALF, HALF)[:1, :count]
    k_label = jnp.where(lane < HALF, own_line, jnp.where(lane < 2 * HALF, far_line, over_line[:1, :count]))
    piece = lane - 2 * HALF
    piece = jnp.where(piece >= EDGE, piece - EDGE, piece)
    spot = jnp.where(lane < HALF, lane, jnp.where(lane < 2 * HALF, lane - HALF, piece))
    if e == 0:
        mine = spot < HALF // 2
    else:
        mine = spot >= jnp.where(lane < 2 * HALF, HALF // 2, EDGE - HALF // 2)
    k_label = jnp.where(mine, k_label, -1.0)
    at = 32 * e
    q = qkv[s, last, :, :D].astype(F32)[at : at + EDGE]
    q_label = qlab[s, last * HALF : SIDE, :][at : at + EDGE, :1]
    return attention(q, keys[0], keys[1], q_label, k_label)


def outer_kernel(
    pay1, pay2, far1, far2, over1, over2, corner, qlab, qkv, kv_edge, mixed, back, gain, bias, w_qkv, b_qkv, w_out, b_out, out
):
    g, b = gain[...].reshape(1, D), bias[...].reshape(1, D)
    kv1 = project_kv(over1[...].astype(F32), g, b, w_qkv, b_qkv)
    kv2 = project_kv(over2[...].astype(F32), g, b, w_qkv, b_qkv)
    kv3 = project_kv(corner[...].astype(F32), g, b, w_qkv, b_qkv)
    line1, line2 = label_line(over1, 3 * EDGE), label_line(over2, 4 * EDGE)
    line3 = label_line(corner, EDGE)
    lane = iota((8, D), 1)
    first = jnp.where(lane < 2 * HALF + EDGE, shifted(line1, 0, 2 * HALF), shifted(line3, 0, 2 * HALF + EDGE))
    rest = (qlab, qkv, kv_edge)
    z0 = edge_window(1, 0, pay1, far1, [k[: 2 * EDGE] for k in kv2], shifted(line2, 0, 2 * HALF), *rest)
    z1 = edge_window(1, 1, pay2, far2, [k[2 * EDGE : 4 * EDGE] for k in kv2], shifted(line2, 2 * EDGE, 2 * HALF), *rest)
    a1 = edge_window(0, 1, pay2, far2, [k[EDGE : 3 * EDGE] for k in kv1], shifted(line1, EDGE, 2 * HALF), *rest)
    a0_kv = [jnp.concatenate([k1[:EDGE], k3[:EDGE]], axis=0) for k1, k3 in zip(kv1, kv3)]
    a0 = edge_window(0, 0, pay1, far1, a0_kv, first, *rest)
    heads, xs = [], []
    for pay, a, z in ((pay1, a0, z0), (pay2, a1, z1)):
        mid = jnp.where(iota((8, 1), 0) < 4, a[32:], z[:8])
        heads.append(jnp.concatenate([a[:32], mid, z[8:]], axis=0))
        xs.append(pay[:SIDE, :].astype(F32)[3 * HALF :])
    edges = finish(jnp.concatenate(heads, axis=0), jnp.concatenate(xs, axis=0), w_out[...], b_out[...].reshape(1, D))
    edges = edges.astype(F32)
    for s in range(2):
        parts = [mixed[s, m].astype(F32) for m in range(BLOCKS - 1)] + [edges[s * HALF : (s + 1) * HALF]]
        done = mm(back[...], jnp.concatenate(parts, axis=0).astype(BF16)).astype(BF16)
        for l in range(LEV):
            out[pl.ds(side_rows(s, l), SIDE // 2), :] = done[l * (SIDE // 2) : (l + 1) * (SIDE // 2)]


VMEM = pl.BlockSpec(memory_space=pltpu.VMEM)


def cost(flops, moved, exps=0):
    return pl.CostEstimate(flops=flops, bytes_accessed=moved, transcendentals=exps)


def call(kernel, name, outs, args, flops, scratch=(), keep=True):
    make = pltpu.VMEM if keep else jax.ShapeDtypeStruct
    return pl.pallas_call(
        kernel,
        out_shape=[make(shape, dtype) for shape, dtype in outs],
        in_specs=[VMEM] * len(args),
        out_specs=[VMEM] * len(outs),
        scratch_shapes=list(scratch),
        compiler_params=pltpu.CompilerParams(vmem_limit_bytes=LIMIT),
        cost_estimate=cost(flops, 4_000_000, 500_000),
        name=name,
    )(*args)


def held(x):
    return pltpu.with_memory_space_constraint(x, pltpu.VMEM)


def pairs(axis, first):
    n = lax.axis_size(axis)
    return [(i, (i + 1) % n) for i in range(first, n, 2)]


def swap(block, axis, first):
    route = [way for i, j in pairs(axis, first) for way in ((i, j), (j, i))]
    return held(lax.ppermute(block, axis, route))


def swap_corners(block):
    n_lon, n_lat = lax.axis_size("lon"), lax.axis_size("lat")
    over_lon = {i: j for p in pairs("lon", 1) for i, j in (p, p[::-1])}
    over_lat = {i: j for p in pairs("lat", 1) for i, j in (p, p[::-1])}
    route = []
    for o in range(n_lon):
        for a in range(n_lat):
            to_o, to_a = o, a
            if a % LAT_RUN in (0, LAT_RUN - 1):
                to_o = over_lon[o]
                if o % LON_RUN in (0, LON_RUN - 1):
                    to_a = over_lat[a]
            else:
                to_a = over_lat[a]
            route.append((o * n_lat + a, to_o * n_lat + to_a))
    return held(lax.ppermute(block, ("lon", "lat"), route))


def local(features, region_ids, ln_gain, ln_bias, w_qkv, b_qkv, w_out, b_out):
    feat = features.transpose(0, 2, 1, 3).reshape(2 * SIDE, D)
    ids = region_ids.transpose(2, 0, 1)
    norm = (held(ln_gain), held(ln_bias))
    into = (held(w_qkv), held(b_qkv))
    outof = (held(w_out), held(b_out))
    pay1, pay2, qlab = call(
        prep_kernel,
        "prep",
        [((PAY, D), BF16), ((PAY, D), BF16), ((2, SIDE, 128), F32)],
        (feat, ids),
        200_000_000,
        [pltpu.VMEM((2, 16, 128), F32)],
    )
    pay1, pay2, qlab = held(pay1), held(pay2), held(qlab)
    far2 = swap(pay2, "lon", 0)
    far1 = swap(pay1, "lon", 1)
    (edge1,) = call(
        functools.partial(edge_kernel, 0), "edge1", [((3 * EDGE + 8, D), BF16)], (pay1, pay2, far2), 1_000_000
    )
    over1 = swap(edge1, "lat", 1)
    (qkv,) = call(own_kernel, "own", [((2, BLOCKS, HALF, 3 * D), BF16)], (pay1, pay2, *norm, *into), 900_000_000)
    qkv = held(qkv)
    (edge2,) = call(
        functools.partial(edge_kernel, 1), "edge2", [((4 * EDGE + 16, D), BF16)], (pay1, far1, pay2, far2), 1_000_000
    )
    over2 = swap(edge2, "lat", 0)
    kv_edge, mixed, back = call(
        inner_kernel,
        "inner",
        [((2, HALF, 2 * D), BF16), ((2, BLOCKS - 1, HALF, D), BF16), ((SIDE, SIDE), BF16)],
        (pay1, pay2, far1, far2, qlab, qkv, *norm, *into, *outof),
        3_000_000_000,
        [pltpu.VMEM((2, SIDE, 2 * D), F32)],
    )
    kv_edge, mixed, back = held(kv_edge), held(mixed), held(back)
    (bend,) = call(corner_kernel, "corner", [((EDGE + 8, D), BF16)], (pay1, far1, over1), 1_000_000)
    corner = swap_corners(bend)
    (out,) = call(
        outer_kernel,
        "outer",
        [((2 * SIDE, D), BF16)],
        (pay1, pay2, far1, far2, over1, over2, corner, qlab, qkv, kv_edge, mixed, back, *norm, *into, *outof),
        1_500_000_000,
        keep=False,
    )
    return out.reshape(LEV, COLS, ROWS, D).transpose(0, 2, 1, 3)


def solution(mesh):
    return jax.shard_map(
        local,
        mesh=mesh,
        in_specs=(P(None, "lat", "lon", None), P(None, "lat", "lon"), P(), P(), P(), P(), P(), P()),
        out_specs=P(None, "lat", "lon", None),
        check_vma=False,
    )
```

```python
import functools

import jax
import jax.numpy as jnp
from jax import lax
from jax.experimental import pallas as pl
from jax.experimental.pallas import tpu as pltpu
from jax.sharding import PartitionSpec as P

HEADS = 8
WLAT = 6
WLON = 12
SLAT = 3
SLON = 6
LEV = 2
D = 512
HS = D // HEADS
ROWS = 24
COLS = 12
HALF = WLAT * LEV * SLON
BLOCKS = ROWS // WLAT
SIDE = BLOCKS * HALF
PAY = SIDE + 16
EDGE = 40
LAT_RUN = 4
LON_RUN = 16
F32 = jnp.float32
BF16 = jnp.bfloat16
LIMIT = 24 * 1024 * 1024


def mm(a, b):
    return jnp.dot(a, b, preferred_element_type=F32)


def mm_nt(a, b):
    return lax.dot_general(a, b, (((1,), (1,)), ((), ())), preferred_element_type=F32)


def iota(shape, dim):
    return lax.broadcasted_iota(jnp.int32, shape, dim)


def place_of(n, odd_lat):
    l = jnp.where(n >= SIDE // 2, 1, 0)
    n = n - SIDE // 2 * l
    c = sum(jnp.where(n >= ROWS * q, 1, 0) for q in range(1, SLON))
    i = n - ROWS * c
    top = 3 * HALF + HALF // 2 * odd_lat + 12 * i
    bottom = 3 * HALF + HALF // 2 * (1 - odd_lat) + 12 * (i - (ROWS - SLAT))
    base = jnp.where(i < SLAT, top, jnp.where(i >= ROWS - SLAT, bottom, 12 * (i - SLAT)))
    return base + SLON * l + c, i, LEV * c + l


def layer_norm(x, gain, bias):
    center = x - jnp.mean(x, axis=-1, keepdims=True)
    spread = jnp.mean(center * center, axis=-1, keepdims=True)
    return (center * lax.rsqrt(spread + 1e-05) * gain + bias).astype(BF16)


def side_rows(s, l):
    odd = lax.axis_index("lon") % 2
    half = odd if s == 0 else 1 - odd
    return pl.multiple_of(l * SIDE + half * (SIDE // 2), SIDE // 2)


def prep_kernel(feat, ids, pay1, pay2, qlab, edge1, bend, lab):
    odd_lon = lax.axis_index("lon") % 2
    odd_lat = lax.axis_index("lat") % 2
    first = lax.axis_index("lat") == 0
    place, lat, strip = place_of(iota((1, SIDE), 1), odd_lat)
    order = jnp.where(iota((SIDE, SIDE), 0) == place, 1.0, 0.0)
    spread = jnp.where(iota((128, SIDE), 0) == lat, 1.0, 0.0).astype(BF16)
    from_first = jnp.where((iota((LEV, ROWS), 1) < SLAT) & first, 4.0, 0.0)
    lab[...] = jnp.zeros_like(lab)
    row = iota((HALF, SIDE), 0)
    edge, edge_line = 0.0, 0.0
    for s, pay in enumerate((pay1, pay2)):
        tokens = jnp.concatenate([feat[pl.ds(side_rows(s, l), SIDE // 2), :] for l in range(LEV)], axis=0)
        ordered = mm(order.astype(BF16), tokens)
        pay[:SIDE, :] = ordered.astype(BF16)
        half = odd_lon if s == 0 else 1 - odd_lon
        for c in range(SLON):
            lab[s, LEV * c : LEV * (c + 1), :ROWS] = ids[SLON * half + c].astype(F32) + from_first
        line = mm(lab[s].astype(BF16), spread)
        line = jnp.sum(jnp.where(iota((16, SIDE), 0) == strip, line, 0.0), axis=0, keepdims=True)
        qlab[s] = jnp.broadcast_to(jnp.sum(order * line, axis=-1, keepdims=True), (SIDE, 128))
        line = jnp.broadcast_to(line, (16, SIDE)).astype(BF16)
        ordered_line = jnp.concatenate([mm_nt(line, order.astype(BF16)), jnp.zeros((16, D - SIDE), F32)], axis=1)
        pay[SIDE:, :] = ordered_line.astype(BF16)
        wanted = jnp.where(row - HALF // 2 * s + 3 * HALF == place, 1.0, 0.0)
        wanted = jnp.where((row < HALF // 2) if s == 0 else (row >= HALF // 2), wanted, 0.0).astype(BF16)
        edge = edge + mm(wanted, tokens)
        edge_line = edge_line + mm_nt(line, wanted)
        if s == 0:
            moved = shifted(ordered_line[:8], 3 * HALF, 0)
            bend[...] = jnp.concatenate([ordered[3 * HALF : 3 * HALF + EDGE], moved], axis=0).astype(BF16)
    edge_line = jnp.concatenate([edge_line[:8], jnp.zeros((8, D - HALF), F32)], axis=1)
    edge1[...] = jnp.concatenate([edge, edge_line], axis=0).astype(BF16)


def own_kernel(pay1, pay2, gain, bias, w_qkv, b_qkv, after, qkv):
    del after
    g, b = gain[...].reshape(1, D), bias[...].reshape(1, D)
    for s, pay in enumerate((pay1, pay2)):
        normed = layer_norm(pay[:SIDE, :].astype(F32), g, b)
        for c in range(3):
            cols = slice(c * D, (c + 1) * D)
            part = mm(normed, w_qkv[:, cols]) + b_qkv[cols].reshape(1, D)
            part = part.astype(BF16).astype(F32)
            if c == 0:
                part = part * HS ** (-0.5)
            for m in range(BLOCKS):
                qkv[s, m, :, cols] = part[m * HALF : (m + 1) * HALF].astype(BF16)


def label_line(ref, at):
    return ref[...].astype(F32)[at : at + 8]


def shifted(line, start, to):
    return pltpu.roll(line, (to - start) % D, 1)


def attention(q, k, v, q_label, k_label):
    n = q.shape[0]
    keys = k.shape[0]
    wide = 4 * HS
    allowed = q_label == k_label
    out = []
    col = iota((1, wide), 1)
    for g in range(2):
        cols = slice(g * wide, (g + 1) * wide)
        own = [(col >= h * HS) & (col < (h + 1) * HS) for h in range(4)]
        qg = q[:, cols]
        stacked = jnp.concatenate([jnp.where(o, qg, 0.0) for o in own], axis=0).astype(BF16)
        scores = mm_nt(stacked, k[:, cols])
        scores = jnp.where(allowed[None], scores.reshape(4, n, keys), -1e30)
        top = jnp.max(scores, axis=-1, keepdims=True)
        expd = jnp.exp(scores - top)
        weights = (expd / jnp.sum(expd, axis=-1, keepdims=True)).astype(BF16)
        full = mm(weights.reshape(4 * n, keys), v[:, cols])
        picked = jnp.where(own[0], full[:n], 0.0)
        for h in range(1, 4):
            picked = jnp.where(own[h], full[h * n : (h + 1) * n], picked)
        out.append(picked)
    return jnp.concatenate(out, axis=1)


def finish(heads, x, w_out, b_out):
    projected = (mm(heads.astype(BF16), w_out) + b_out).astype(BF16).astype(F32)
    return (x + projected).astype(BF16)


def edge_piece(ref, e):
    at = 3 * HALF + 32 * e
    return ref[...].astype(F32)[at : at + EDGE]


def edge_labels(parts):
    lane = iota((8, D), 1)
    out = jnp.zeros((8, D), F32)
    for j, (line, start) in enumerate(parts):
        out = jnp.where((lane >= j * EDGE) & (lane < (j + 1) * EDGE), shifted(line, start, j * EDGE), out)
    return out


def corner_piece(ref):
    return jnp.concatenate([edge_piece(ref, 0), shifted(label_line(ref, SIDE), 3 * HALF, 0)], axis=0).astype(BF16)


def second_kernel(pay1, far1, pay2, far2, out, bend):
    refs = (pay1, far1, pay2, far2)
    rows = [edge_piece(ref, 1) for ref in refs]
    line = edge_labels([(label_line(ref, SIDE), 3 * HALF + 32) for ref in refs])
    out[...] = jnp.concatenate([*rows, line, line], axis=0).astype(BF16)
    bend[...] = corner_piece(far1)


def gate_kernel(x, after, out):
    del after
    out[...] = x[...]


def third_kernel(over1, after, first, second):
    del after
    x, line = over1[...].astype(F32), label_line(over1, HALF)
    for out, at in ((first, 0), (second, 32)):
        out[...] = jnp.concatenate([x[at : at + EDGE], shifted(line, at, 0)], axis=0).astype(BF16)


def inner_kernel(pay1, pay2, far1, far2, qlab, qkv, gain, bias, w_qkv, b_qkv, w_out, b_out, kv_edge, mixed, back, kv):
    g, b = gain[...].reshape(1, D), bias[...].reshape(1, D)
    for s, far in enumerate((far1, far2)):
        normed = layer_norm(far[:SIDE, :].astype(F32), g, b)
        for c in range(2):
            cols = slice((c + 1) * D, (c + 2) * D)
            part = mm(normed, w_qkv[:, cols]) + b_qkv[cols].reshape(1, D)
            kv[s, :, c * D : (c + 1) * D] = part
            kv_edge[s, :, c * D : (c + 1) * D] = part[3 * HALF :].astype(BF16)
    place, _, _ = place_of(iota((SIDE, 1), 0), lax.axis_index("lat") % 2)
    back[...] = jnp.where(iota((SIDE, SIDE), 1) == place, 1.0, 0.0).astype(BF16)
    for m in range(BLOCKS - 1):
        rows = slice(m * HALF, (m + 1) * HALF)
        heads, xs = [], []
        for s, (pay, far) in enumerate(((pay1, far1), (pay2, far2))):
            both = jnp.concatenate([qkv[s, m, :, D:].astype(F32), kv[s, rows, :]], axis=0).astype(BF16)
            own_line = shifted(label_line(pay, SIDE), m * HALF, 0)[:1, : 2 * HALF]
            far_line = shifted(label_line(far, SIDE), m * HALF, HALF)[:1, : 2 * HALF]
            k_label = jnp.where(iota((1, 2 * HALF), 1) < HALF, own_line, far_line)
            q_label = qlab[s, rows, :][:, :1]
            heads.append(attention(qkv[s, m, :, :D].astype(F32), both[:, :D], both[:, D:], q_label, k_label))
            xs.append(pay[:SIDE, :].astype(F32)[rows])
        done = finish(jnp.concatenate(heads, axis=0), jnp.concatenate(xs, axis=0), w_out[...], b_out[...].reshape(1, D))
        mixed[0, m] = done[:HALF]
        mixed[1, m] = done[HALF:]


def project_kv(x, g, b, w_qkv, b_qkv):
    normed = layer_norm(x, g, b)
    return [
        mm(normed, w_qkv[:, (c + 1) * D : (c + 2) * D]) + b_qkv[(c + 1) * D : (c + 2) * D].reshape(1, D) for c in range(2)
    ]


def edge_window(e, s, pay, far, over_kv, over_line, late, qlab, qkv, kv_edge):
    last = BLOCKS - 1
    keys = []
    for c in range(2):
        own = qkv[s, last, :, (c + 1) * D : (c + 2) * D].astype(F32)
        far_part = kv_edge[s, :, c * D : (c + 1) * D].astype(F32)
        keys.append(jnp.concatenate([own, far_part, over_kv[c]], axis=0).astype(BF16))
    count = 2 * HALF + 2 * EDGE
    lane = iota((1, count), 1)
    own_line = shifted(label_line(pay, SIDE), last * HALF, 0)[:1, :count]
    far_line = shifted(label_line(far, SIDE), last * HALF, HALF)[:1, :count]
    k_label = jnp.where(lane < HALF, own_line, jnp.where(lane < 2 * HALF, far_line, over_line[:1, :count]))
    piece = lane - 2 * HALF
    piece = jnp.where(piece >= EDGE, piece - EDGE, piece)
    spot = jnp.where(lane < HALF, lane, jnp.where(lane < 2 * HALF, lane - HALF, piece))
    from_row = jnp.where(lane < 2 * HALF, HALF // 2 * e, EDGE - HALF // 2 if late else 0)
    mine = (spot >= from_row) & (spot < from_row + HALF // 2)
    k_label = jnp.where(mine, k_label, -1.0)
    at = 32 * e
    q = qkv[s, last, :, :D].astype(F32)[at : at + EDGE]
    q_label = qlab[s, last * HALF : SIDE, :][at : at + EDGE, :1]
    return attention(q, keys[0], keys[1], q_label, k_label)


def near_kernel(pay1, pay2, far1, far2, over2, qlab, qkv, kv_edge, gain, bias, w_qkv, b_qkv, out):
    g, b = gain[...].reshape(1, D), bias[...].reshape(1, D)
    kv = project_kv(over2[...].astype(F32), g, b, w_qkv, b_qkv)
    line = label_line(over2, 4 * EDGE)
    for s, (pay, far) in enumerate(((pay1, far1), (pay2, far2))):
        part = [k[2 * EDGE * s : 2 * EDGE * (s + 1)] for k in kv]
        out[s] = edge_window(1, s, pay, far, part, shifted(line, 2 * EDGE * s, 2 * HALF), True, qlab, qkv, kv_edge)


def outer_kernel(
    pay1, pay2, far1, far2, over1, bend1, bend2, bend3, bend4, near, qlab, qkv, kv_edge, mixed, back, gain, bias, w_qkv, b_qkv, w_out, b_out, out
):
    g, b = gain[...].reshape(1, D), bias[...].reshape(1, D)
    corner = bend1[...].astype(F32) + bend2[...].astype(F32) + bend3[...].astype(F32)
    other = bend4[...].astype(F32)
    kv = project_kv(jnp.concatenate([over1[...].astype(F32), corner, other], axis=0), g, b, w_qkv, b_qkv)
    line = label_line(over1, HALF)
    lane = iota((8, D), 1)
    rest = (qlab, qkv, kv_edge)
    at = over1.shape[0]
    a = []
    for s, (pay, far, bent) in enumerate(((pay1, far1, corner), (pay2, far2, other))):
        kv_s = [jnp.concatenate([k[32 * s : 32 * s + EDGE], k[at : at + EDGE]], axis=0) for k in kv]
        mine, theirs = shifted(line, 32 * s, 2 * HALF), shifted(bent[EDGE:], 0, 2 * HALF + EDGE)
        line_s = jnp.where(lane < 2 * HALF + EDGE, mine, theirs)
        a.append(edge_window(0, s, pay, far, kv_s, line_s, s == 1, *rest))
        at += EDGE + 8
    heads, xs = [], []
    for s, pay in enumerate((pay1, pay2)):
        z = near[s]
        mid = jnp.where(iota((8, 1), 0) < 4, a[s][32:], z[:8])
        heads.append(jnp.concatenate([a[s][:32], mid, z[8:]], axis=0))
        xs.append(pay[:SIDE, :].astype(F32)[3 * HALF :])
    edges = finish(jnp.concatenate(heads, axis=0), jnp.concatenate(xs, axis=0), w_out[...], b_out[...].reshape(1, D))
    edges = edges.astype(F32)
    for s in range(2):
        parts = [mixed[s, m].astype(F32) for m in range(BLOCKS - 1)] + [edges[s * HALF : (s + 1) * HALF]]
        done = mm(back[...], jnp.concatenate(parts, axis=0).astype(BF16)).astype(BF16)
        for l in range(LEV):
            out[pl.ds(side_rows(s, l), SIDE // 2), :] = done[l * (SIDE // 2) : (l + 1) * (SIDE // 2)]


VMEM = pl.BlockSpec(memory_space=pltpu.VMEM)


def cost(flops, moved, exps=0):
    return pl.CostEstimate(flops=flops, bytes_accessed=moved, transcendentals=exps)


def call(kernel, name, outs, args, flops, scratch=(), keep=True):
    make = pltpu.VMEM if keep else jax.ShapeDtypeStruct
    return pl.pallas_call(
        kernel,
        out_shape=[make(shape, dtype) for shape, dtype in outs],
        in_specs=[VMEM] * len(args),
        out_specs=[VMEM] * len(outs),
        scratch_shapes=list(scratch),
        compiler_params=pltpu.CompilerParams(vmem_limit_bytes=LIMIT),
        cost_estimate=cost(flops, 4_000_000, 500_000),
        name=name,
    )(*args)


def held(x):
    return pltpu.with_memory_space_constraint(x, pltpu.VMEM)


def gate(x, after):
    return held(call(gate_kernel, "gate", [(x.shape, x.dtype)], (held(x), after), 1_000)[0])


def pairs(axis, first):
    n = lax.axis_size(axis)
    return [(i, (i + 1) % n) for i in range(first, n, 2)]


def swap(block, axis, first):
    route = [way for i, j in pairs(axis, first) for way in ((i, j), (j, i))]
    return held(lax.ppermute(block, axis, route))


def swap_corners(block, way):
    n_lon, n_lat = lax.axis_size("lon"), lax.axis_size("lat")
    over_lon = {i: j for p in pairs("lon", 1) for i, j in (p, p[::-1])}
    over_lat = {i: j for p in pairs("lat", 1) for i, j in (p, p[::-1])}
    route = []
    for o in range(n_lon):
        for a in range(n_lat):
            far_lat = a % LAT_RUN in (0, LAT_RUN - 1)
            far_lon = o % LON_RUN in (0, LON_RUN - 1)
            if way == ("direct" if far_lat and far_lon else "lon" if far_lat else "lat"):
                to = (o if way == "lat" else over_lon[o]) * n_lat + (a if way == "lon" else over_lat[a])
                route.append((o * n_lat + a, to))
    return held(lax.ppermute(block, ("lon", "lat"), route))


def local(features, region_ids, ln_gain, ln_bias, w_qkv, b_qkv, w_out, b_out):
    feat = features.transpose(0, 2, 1, 3).reshape(2 * SIDE, D)
    ids = region_ids.transpose(2, 0, 1)
    norm = (held(ln_gain), held(ln_bias))
    into = (held(w_qkv), held(b_qkv))
    outof = (held(w_out), held(b_out))
    pay1, pay2, qlab, edge1, bend = call(
        prep_kernel,
        "prep",
        [((PAY, D), BF16), ((PAY, D), BF16), ((2, SIDE, 128), F32), ((HALF + 8, D), BF16), ((EDGE + 8, D), BF16)],
        (feat, ids),
        200_000_000,
        [pltpu.VMEM((2, 16, 128), F32)],
    )
    pay1, pay2, qlab = held(pay1), held(pay2), held(qlab)
    far2 = swap(pay2, "lon", 0)
    far1 = swap(pay1, "lon", 1)
    edge1 = gate(edge1, far2)
    over1 = swap(edge1, "lat", 1)
    bend = gate(bend, edge1)
    bend1 = swap_corners(bend, "direct")
    (qkv,) = call(own_kernel, "own", [((2, BLOCKS, HALF, 3 * D), BF16)], (pay1, pay2, *norm, *into, bend), 900_000_000)
    qkv = held(qkv)
    edge2, bend = call(
        second_kernel,
        "edge2",
        [((4 * EDGE + 16, D), BF16), ((EDGE + 8, D), BF16)],
        (pay1, far1, pay2, far2),
        1_000_000,
    )
    bend2 = swap_corners(bend, "lat")
    over2 = swap(edge2, "lat", 0)
    kv_edge, mixed, back = call(
        inner_kernel,
        "inner",
        [((2, HALF, 2 * D), BF16), ((2, BLOCKS - 1, HALF, D), BF16), ((SIDE, SIDE), BF16)],
        (pay1, pay2, far1, far2, qlab, qkv, *norm, *into, *outof),
        3_000_000_000,
        [pltpu.VMEM((2, SIDE, 2 * D), F32)],
    )
    kv_edge, mixed, back = held(kv_edge), held(mixed), held(back)
    (near,) = call(
        near_kernel,
        "near",
        [((2, EDGE, D), F32)],
        (pay1, pay2, far1, far2, over2, qlab, qkv, kv_edge, *norm, *into),
        1_000_000_000,
    )
    bend, other = call(third_kernel, "third", [((EDGE + 8, D), BF16)] * 2, (over1, kv_edge), 1_000_000)
    bend3 = swap_corners(bend, "lon")
    bend4 = swap(other, "lon", 0)
    (out,) = call(
        outer_kernel,
        "outer",
        [((2 * SIDE, D), BF16)],
        (
            *(pay1, pay2, far1, far2, over1, bend1, bend2, bend3, bend4, held(near)),
            *(qlab, qkv, kv_edge, mixed, back, *norm, *into, *outof),
        ),
        1_500_000_000,
        keep=False,
    )
    return out.reshape(LEV, COLS, ROWS, D).transpose(0, 2, 1, 3)


def solution(mesh):
    return jax.shard_map(
        local,
        mesh=mesh,
        in_specs=(P(None, "lat", "lon", None), P(None, "lat", "lon"), P(), P(), P(), P(), P(), P()),
        out_specs=P(None, "lat", "lon", None),
        check_vma=False,
    )
```

```python
import functools

import jax
import jax.numpy as jnp
from jax import lax
from jax.experimental import pallas as pl
from jax.experimental.pallas import tpu as pltpu
from jax.sharding import PartitionSpec as P

HEADS = 8
WLAT = 6
WLON = 12
SLAT = 3
SLON = 6
LEV = 2
D = 512
HS = D // HEADS
ROWS = 24
COLS = 12
HALF = WLAT * LEV * SLON
BLOCKS = ROWS // WLAT
SIDE = BLOCKS * HALF
PAY = SIDE + 16
EDGE = 40
LAT_RUN = 4
LON_RUN = 16
F32 = jnp.float32
BF16 = jnp.bfloat16
LIMIT = 24 * 1024 * 1024


def mm(a, b):
    return jnp.dot(a, b, preferred_element_type=F32)


def mm_nt(a, b):
    return lax.dot_general(a, b, (((1,), (1,)), ((), ())), preferred_element_type=F32)


def iota(shape, dim):
    return lax.broadcasted_iota(jnp.int32, shape, dim)


def place_of(n, odd_lat):
    l = jnp.where(n >= SIDE // 2, 1, 0)
    n = n - SIDE // 2 * l
    c = sum(jnp.where(n >= ROWS * q, 1, 0) for q in range(1, SLON))
    i = n - ROWS * c
    top = 3 * HALF + HALF // 2 * odd_lat + 12 * i
    bottom = 3 * HALF + HALF // 2 * (1 - odd_lat) + 12 * (i - (ROWS - SLAT))
    base = jnp.where(i < SLAT, top, jnp.where(i >= ROWS - SLAT, bottom, 12 * (i - SLAT)))
    return base + SLON * l + c, i, LEV * c + l


def layer_norm(x, gain, bias):
    center = x - jnp.mean(x, axis=-1, keepdims=True)
    spread = jnp.mean(center * center, axis=-1, keepdims=True)
    return (center * lax.rsqrt(spread + 1e-05) * gain + bias).astype(BF16)


def side_rows(s, l):
    odd = lax.axis_index("lon") % 2
    half = odd if s == 0 else 1 - odd
    return pl.multiple_of(l * SIDE + half * (SIDE // 2), SIDE // 2)


def prep_kernel(*refs):
    refs, (pay1, pay2, qlab, edge1, bend), weights, (lab, feat, ids, sem) = refs[:8], refs[8:13], refs[13:19], refs[19:]
    copies = [pltpu.make_async_copy(a, b, sem.at[i]) for i, (a, b) in enumerate(zip(refs, (feat, ids, *weights)))]
    for copy in copies:
        copy.start()
    odd_lon = lax.axis_index("lon") % 2
    odd_lat = lax.axis_index("lat") % 2
    first = lax.axis_index("lat") == 0
    place, lat, strip = place_of(iota((1, SIDE), 1), odd_lat)
    order = jnp.where(iota((SIDE, SIDE), 0) == place, 1.0, 0.0)
    spread = jnp.where(iota((128, SIDE), 0) == lat, 1.0, 0.0).astype(BF16)
    from_first = jnp.where((iota((LEV, ROWS), 1) < SLAT) & first, 4.0, 0.0)
    lab[...] = jnp.zeros_like(lab)
    row = iota((HALF, SIDE), 0)
    edge, edge_line = 0.0, 0.0
    for copy in copies[:2]:
        copy.wait()
    for s, pay in enumerate((pay1, pay2)):
        tokens = jnp.concatenate([feat[pl.ds(side_rows(s, l), SIDE // 2), :] for l in range(LEV)], axis=0)
        ordered = mm(order.astype(BF16), tokens)
        pay[:SIDE, :] = ordered.astype(BF16)
        half = odd_lon if s == 0 else 1 - odd_lon
        for c in range(SLON):
            lab[s, LEV * c : LEV * (c + 1), :ROWS] = ids[SLON * half + c].astype(F32) + from_first
        line = mm(lab[s].astype(BF16), spread)
        line = jnp.sum(jnp.where(iota((16, SIDE), 0) == strip, line, 0.0), axis=0, keepdims=True)
        qlab[s] = jnp.broadcast_to(jnp.sum(order * line, axis=-1, keepdims=True), (SIDE, 128))
        line = jnp.broadcast_to(line, (16, SIDE)).astype(BF16)
        ordered_line = jnp.concatenate([mm_nt(line, order.astype(BF16)), jnp.zeros((16, D - SIDE), F32)], axis=1)
        pay[SIDE:, :] = ordered_line.astype(BF16)
        wanted = jnp.where(row - HALF // 2 * s + 3 * HALF == place, 1.0, 0.0)
        wanted = jnp.where((row < HALF // 2) if s == 0 else (row >= HALF // 2), wanted, 0.0).astype(BF16)
        edge = edge + mm(wanted, tokens)
        edge_line = edge_line + mm_nt(line, wanted)
        if s == 0:
            moved = shifted(ordered_line[:8], 3 * HALF, 0)
            bend[...] = jnp.concatenate([ordered[3 * HALF : 3 * HALF + EDGE], moved], axis=0).astype(BF16)
    edge_line = jnp.concatenate([edge_line[:8], jnp.zeros((8, D - HALF), F32)], axis=1)
    edge1[...] = jnp.concatenate([edge, edge_line], axis=0).astype(BF16)
    for copy in copies[2:]:
        copy.wait()


def own_part(pay1, pay2, gain, bias, w_qkv, b_qkv, qkv, back):
    g, b = gain[...].reshape(1, D), bias[...].reshape(1, D)
    for s, pay in enumerate((pay1, pay2)):
        normed = layer_norm(pay[:SIDE, :].astype(F32), g, b)
        for c in range(3):
            cols = slice(c * D, (c + 1) * D)
            part = mm(normed, w_qkv[:, cols]) + b_qkv[cols].reshape(1, D)
            part = part.astype(BF16).astype(F32)
            if c == 0:
                part = part * HS ** (-0.5)
            for m in range(BLOCKS):
                qkv[s, m, :, cols] = part[m * HALF : (m + 1) * HALF].astype(BF16)
    place, _, _ = place_of(iota((SIDE, 1), 0), lax.axis_index("lat") % 2)
    back[...] = jnp.where(iota((SIDE, SIDE), 1) == place, 1.0, 0.0).astype(BF16)


def soon():
    return (lax.axis_index("lat") < LAT_RUN) & (lax.axis_index("lon") % LON_RUN < 6)


def ahead_kernel(pay1, pay2, *refs):
    qkv, back, _, _ = refs[-4:]

    @pl.when(soon())
    def _():
        own_part(pay1, pay2, *refs[:-4], qkv, back)


def own_kernel(pay1, pay2, gain, bias, w_qkv, b_qkv, after, qkv_in, back_in, qkv, back):
    del after, qkv_in, back_in

    @pl.when(jnp.logical_not(soon()))
    def _():
        own_part(pay1, pay2, gain, bias, w_qkv, b_qkv, qkv, back)


def label_line(ref, at):
    return ref[...].astype(F32)[at : at + 8]


def shifted(line, start, to):
    return pltpu.roll(line, (to - start) % D, 1)


def attention(q, k, v, q_label, k_label):
    n = q.shape[0]
    keys = k.shape[0]
    wide = 4 * HS
    allowed = q_label == k_label
    out = []
    col = iota((1, wide), 1)
    for g in range(2):
        cols = slice(g * wide, (g + 1) * wide)
        own = [(col >= h * HS) & (col < (h + 1) * HS) for h in range(4)]
        qg = q[:, cols]
        stacked = jnp.concatenate([jnp.where(o, qg, 0.0) for o in own], axis=0).astype(BF16)
        scores = mm_nt(stacked, k[:, cols])
        scores = jnp.where(allowed[None], scores.reshape(4, n, keys), -1e30).reshape(4 * n, keys)
        expd = jnp.exp(scores - jnp.max(scores, axis=-1, keepdims=True))
        full = mm(expd.astype(BF16), v[:, cols])
        share = 1.0 / jnp.sum(expd, axis=-1, keepdims=True)
        picked = full[:n] * share[:n]
        for h in range(1, 4):
            rows = slice(h * n, (h + 1) * n)
            picked = jnp.where(own[h], full[rows] * share[rows], picked)
        out.append(picked)
    return jnp.concatenate(out, axis=1)


def finish(heads, x, w_out, b_out):
    projected = (mm(heads.astype(BF16), w_out) + b_out).astype(BF16).astype(F32)
    return (x + projected).astype(BF16)


def edge_piece(ref, e):
    at = 3 * HALF + 32 * e
    return ref[...].astype(F32)[at : at + EDGE]


def edge_labels(parts):
    lane = iota((8, D), 1)
    out = jnp.zeros((8, D), F32)
    for j, (line, start) in enumerate(parts):
        out = jnp.where((lane >= j * EDGE) & (lane < (j + 1) * EDGE), shifted(line, start, j * EDGE), out)
    return out


def corner_piece(ref):
    return jnp.concatenate([edge_piece(ref, 0), shifted(label_line(ref, SIDE), 3 * HALF, 0)], axis=0).astype(BF16)


def second_kernel(pay1, far1, pay2, far2, out, bend):
    refs = (pay1, far1, pay2, far2)
    rows = [edge_piece(ref, 1) for ref in refs]
    line = edge_labels([(label_line(ref, SIDE), 3 * HALF + 32) for ref in refs])
    out[...] = jnp.concatenate([*rows, line, line], axis=0).astype(BF16)
    bend[...] = corner_piece(far1)


def gate_kernel(x, after, out):
    del after
    out[...] = x[...]


def third_kernel(over1, after, first, second):
    del after
    x, line = over1[...].astype(F32), label_line(over1, HALF)
    for out, at in ((first, 0), (second, 32)):
        out[...] = jnp.concatenate([x[at : at + EDGE], shifted(line, at, 0)], axis=0).astype(BF16)


def inner_kernel(pay1, pay2, far1, far2, qlab, qkv, gain, bias, w_qkv, b_qkv, w_out, b_out, kv_edge, mixed, kv):
    g, b = gain[...].reshape(1, D), bias[...].reshape(1, D)
    for s, far in enumerate((far1, far2)):
        normed = layer_norm(far[:SIDE, :].astype(F32), g, b)
        for c in range(2):
            cols = slice((c + 1) * D, (c + 2) * D)
            part = mm(normed, w_qkv[:, cols]) + b_qkv[cols].reshape(1, D)
            kv[s, :, c * D : (c + 1) * D] = part
            kv_edge[s, :, c * D : (c + 1) * D] = part[3 * HALF :].astype(BF16)
    for m in range(BLOCKS - 1):
        rows = slice(m * HALF, (m + 1) * HALF)
        heads, xs = [], []
        for s, (pay, far) in enumerate(((pay1, far1), (pay2, far2))):
            both = jnp.concatenate([qkv[s, m, :, D:].astype(F32), kv[s, rows, :]], axis=0).astype(BF16)
            own_line = shifted(label_line(pay, SIDE), m * HALF, 0)[:1, : 2 * HALF]
            far_line = shifted(label_line(far, SIDE), m * HALF, HALF)[:1, : 2 * HALF]
            k_label = jnp.where(iota((1, 2 * HALF), 1) < HALF, own_line, far_line)
            q_label = qlab[s, rows, :][:, :1]
            heads.append(attention(qkv[s, m, :, :D].astype(F32), both[:, :D], both[:, D:], q_label, k_label))
            xs.append(pay[:SIDE, :].astype(F32)[rows])
        done = finish(jnp.concatenate(heads, axis=0), jnp.concatenate(xs, axis=0), w_out[...], b_out[...].reshape(1, D))
        mixed[0, m] = done[:HALF]
        mixed[1, m] = done[HALF:]


def project_kv(x, g, b, w_qkv, b_qkv):
    normed = layer_norm(x, g, b)
    return [
        mm(normed, w_qkv[:, (c + 1) * D : (c + 2) * D]) + b_qkv[(c + 1) * D : (c + 2) * D].reshape(1, D) for c in range(2)
    ]


def edge_window(e, s, pay, far, over_kv, over_line, late, qlab, qkv, kv_edge):
    last = BLOCKS - 1
    keys = []
    for c in range(2):
        own = qkv[s, last, :, (c + 1) * D : (c + 2) * D].astype(F32)
        far_part = kv_edge[s, :, c * D : (c + 1) * D].astype(F32)
        keys.append(jnp.concatenate([own, far_part, over_kv[c]], axis=0).astype(BF16))
    count = 2 * HALF + 2 * EDGE
    lane = iota((1, count), 1)
    own_line = shifted(label_line(pay, SIDE), last * HALF, 0)[:1, :count]
    far_line = shifted(label_line(far, SIDE), last * HALF, HALF)[:1, :count]
    k_label = jnp.where(lane < HALF, own_line, jnp.where(lane < 2 * HALF, far_line, over_line[:1, :count]))
    piece = lane - 2 * HALF
    piece = jnp.where(piece >= EDGE, piece - EDGE, piece)
    spot = jnp.where(lane < HALF, lane, jnp.where(lane < 2 * HALF, lane - HALF, piece))
    from_row = jnp.where(lane < 2 * HALF, HALF // 2 * e, EDGE - HALF // 2 if late else 0)
    mine = (spot >= from_row) & (spot < from_row + HALF // 2)
    k_label = jnp.where(mine, k_label, -1.0)
    at = 32 * e
    q = qkv[s, last, :, :D].astype(F32)[at : at + EDGE]
    q_label = qlab[s, last * HALF : SIDE, :][at : at + EDGE, :1]
    return attention(q, keys[0], keys[1], q_label, k_label)


def near_kernel(pay1, pay2, far1, far2, over2, qlab, qkv, kv_edge, gain, bias, w_qkv, b_qkv, out):
    g, b = gain[...].reshape(1, D), bias[...].reshape(1, D)
    kv = project_kv(over2[...].astype(F32), g, b, w_qkv, b_qkv)
    line = label_line(over2, 4 * EDGE)
    for s, (pay, far) in enumerate(((pay1, far1), (pay2, far2))):
        part = [k[2 * EDGE * s : 2 * EDGE * (s + 1)] for k in kv]
        out[s] = edge_window(1, s, pay, far, part, shifted(line, 2 * EDGE * s, 2 * HALF), True, qlab, qkv, kv_edge)


def outer_kernel(
    pay1, pay2, far1, far2, over1, bend1, bend2, bend3, bend4, near, qlab, qkv, kv_edge, mixed, back, gain, bias, w_qkv, b_qkv, w_out, b_out, out
):
    g, b = gain[...].reshape(1, D), bias[...].reshape(1, D)
    corner = bend1[...].astype(F32) + bend2[...].astype(F32) + bend3[...].astype(F32)
    other = bend4[...].astype(F32)
    kv = project_kv(jnp.concatenate([over1[...].astype(F32), corner, other], axis=0), g, b, w_qkv, b_qkv)
    line = label_line(over1, HALF)
    lane = iota((8, D), 1)
    rest = (qlab, qkv, kv_edge)
    at = over1.shape[0]
    a = []
    for s, (pay, far, bent) in enumerate(((pay1, far1, corner), (pay2, far2, other))):
        kv_s = [jnp.concatenate([k[32 * s : 32 * s + EDGE], k[at : at + EDGE]], axis=0) for k in kv]
        mine, theirs = shifted(line, 32 * s, 2 * HALF), shifted(bent[EDGE:], 0, 2 * HALF + EDGE)
        line_s = jnp.where(lane < 2 * HALF + EDGE, mine, theirs)
        a.append(edge_window(0, s, pay, far, kv_s, line_s, s == 1, *rest))
        at += EDGE + 8
    heads, xs = [], []
    for s, pay in enumerate((pay1, pay2)):
        z = near[s]
        mid = jnp.where(iota((8, 1), 0) < 4, a[s][32:], z[:8])
        heads.append(jnp.concatenate([a[s][:32], mid, z[8:]], axis=0))
        xs.append(pay[:SIDE, :].astype(F32)[3 * HALF :])
    edges = finish(jnp.concatenate(heads, axis=0), jnp.concatenate(xs, axis=0), w_out[...], b_out[...].reshape(1, D))
    edges = edges.astype(F32)
    for s in range(2):
        parts = [mixed[s, m].astype(F32) for m in range(BLOCKS - 1)] + [edges[s * HALF : (s + 1) * HALF]]
        done = mm(back[...], jnp.concatenate(parts, axis=0).astype(BF16)).astype(BF16)
        for l in range(LEV):
            out[pl.ds(side_rows(s, l), SIDE // 2), :] = done[l * (SIDE // 2) : (l + 1) * (SIDE // 2)]


VMEM = pl.BlockSpec(memory_space=pltpu.VMEM)


def cost(flops, moved, exps=0):
    return pl.CostEstimate(flops=flops, bytes_accessed=moved, transcendentals=exps)


def call(kernel, name, outs, args, flops, scratch=(), keep=True, spec=VMEM, aliases=()):
    make = pltpu.VMEM if keep else jax.ShapeDtypeStruct
    return pl.pallas_call(
        kernel,
        out_shape=[make(shape, dtype) for shape, dtype in outs],
        in_specs=[spec] * len(args),
        out_specs=[VMEM] * len(outs),
        scratch_shapes=list(scratch),
        input_output_aliases=dict(aliases),
        compiler_params=pltpu.CompilerParams(vmem_limit_bytes=LIMIT),
        cost_estimate=cost(flops, 4_000_000, 500_000),
        name=name,
    )(*args)


def held(x):
    return pltpu.with_memory_space_constraint(x, pltpu.VMEM)


def gate(x, after):
    return held(call(gate_kernel, "gate", [(x.shape, x.dtype)], (held(x), after), 1_000)[0])


def pairs(axis, first):
    n = lax.axis_size(axis)
    return [(i, (i + 1) % n) for i in range(first, n, 2)]


def swap(block, axis, first):
    route = [way for i, j in pairs(axis, first) for way in ((i, j), (j, i))]
    return held(lax.ppermute(block, axis, route))


def swap_corners(block, way):
    n_lon, n_lat = lax.axis_size("lon"), lax.axis_size("lat")
    over_lon = {i: j for p in pairs("lon", 1) for i, j in (p, p[::-1])}
    over_lat = {i: j for p in pairs("lat", 1) for i, j in (p, p[::-1])}
    route = []
    for o in range(n_lon):
        for a in range(n_lat):
            far_lat = a % LAT_RUN in (0, LAT_RUN - 1)
            far_lon = o % LON_RUN in (0, LON_RUN - 1)
            if way == ("direct" if far_lat and far_lon else "lon" if far_lat else "lat"):
                to = (o if way == "lat" else over_lon[o]) * n_lat + (a if way == "lon" else over_lat[a])
                route.append((o * n_lat + a, to))
    return held(lax.ppermute(block, ("lon", "lat"), route))


def local(features, region_ids, ln_gain, ln_bias, w_qkv, b_qkv, w_out, b_out):
    feat = features.transpose(0, 2, 1, 3).reshape(2 * SIDE, D)
    ids = region_ids.transpose(2, 0, 1)
    weights = (ln_gain, ln_bias, w_qkv, b_qkv, w_out, b_out)
    pay1, pay2, qlab, edge1, bend, *weights = call(
        prep_kernel,
        "prep",
        [
            *[((PAY, D), BF16), ((PAY, D), BF16), ((2, SIDE, 128), F32), ((HALF + 8, D), BF16), ((EDGE + 8, D), BF16)],
            *[(w.shape, w.dtype) for w in weights],
        ],
        [pltpu.with_memory_space_constraint(x, pltpu.HBM) for x in (feat, ids, *weights)],
        200_000_000,
        [
            pltpu.VMEM((2, 16, 128), F32),
            pltpu.VMEM(feat.shape, BF16),
            pltpu.VMEM(ids.shape, jnp.int32),
            pltpu.SemaphoreType.DMA((8,)),
        ],
        spec=pl.BlockSpec(memory_space=pl.ANY),
    )
    weights = [held(w) for w in weights]
    norm, into, outof = weights[:2], weights[2:4], weights[4:]
    qkv_back = [((2, BLOCKS, HALF, 3 * D), BF16), ((SIDE, SIDE), BF16)]
    qkv, back, pay1, pay2 = call(
        ahead_kernel,
        "ahead",
        [*qkv_back, ((PAY, D), BF16), ((PAY, D), BF16)],
        (held(pay1), held(pay2), *norm, *into),
        900_000_000,
        aliases={0: 2, 1: 3},
    )
    pay1, pay2, qlab = held(pay1), held(pay2), held(qlab)
    far2 = swap(pay2, "lon", 0)
    far1 = swap(pay1, "lon", 1)
    edge1 = gate(edge1, far2)
    over1 = swap(edge1, "lat", 1)
    bend = gate(bend, edge1)
    bend1 = swap_corners(bend, "direct")
    args = (pay1, pay2, *norm, *into, far1, held(qkv), held(back))
    qkv, back = call(own_kernel, "own", qkv_back, args, 900_000_000, aliases={7: 0, 8: 1})
    qkv, back = held(qkv), held(back)
    edge2, bend = call(
        second_kernel,
        "edge2",
        [((4 * EDGE + 16, D), BF16), ((EDGE + 8, D), BF16)],
        (pay1, far1, pay2, far2),
        1_000_000,
    )
    bend2 = swap_corners(bend, "lat")
    over2 = swap(edge2, "lat", 0)
    kv_edge, mixed = call(
        inner_kernel,
        "inner",
        [((2, HALF, 2 * D), BF16), ((2, BLOCKS - 1, HALF, D), BF16)],
        (pay1, pay2, far1, far2, qlab, qkv, *norm, *into, *outof),
        3_000_000_000,
        [pltpu.VMEM((2, SIDE, 2 * D), F32)],
    )
    kv_edge, mixed = held(kv_edge), held(mixed)
    (near,) = call(
        near_kernel,
        "near",
        [((2, EDGE, D), F32)],
        (pay1, pay2, far1, far2, over2, qlab, qkv, kv_edge, *norm, *into),
        1_000_000_000,
    )
    bend, other = call(third_kernel, "third", [((EDGE + 8, D), BF16)] * 2, (over1, kv_edge), 1_000_000)
    bend3 = swap_corners(bend, "lon")
    bend4 = swap(other, "lon", 0)
    (out,) = call(
        outer_kernel,
        "outer",
        [((2 * SIDE, D), BF16)],
        (
            *(pay1, pay2, far1, far2, over1, bend1, bend2, bend3, bend4, held(near)),
            *(qlab, qkv, kv_edge, mixed, back, *norm, *into, *outof),
        ),
        1_500_000_000,
        keep=False,
    )
    return out.reshape(LEV, COLS, ROWS, D).transpose(0, 2, 1, 3)


def solution(mesh):
    return jax.shard_map(
        local,
        mesh=mesh,
        in_specs=(P(None, "lat", "lon", None), P(None, "lat", "lon"), P(), P(), P(), P(), P(), P()),
        out_specs=P(None, "lat", "lon", None),
        check_vma=False,
    )
```

```python
import functools

import jax
import jax.numpy as jnp
from jax import lax
from jax.experimental import pallas as pl
from jax.experimental.pallas import tpu as pltpu
from jax.sharding import PartitionSpec as P

HEADS = 8
WLAT = 6
WLON = 12
SLAT = 3
SLON = 6
LEV = 2
D = 512
HS = D // HEADS
ROWS = 24
COLS = 12
HALF = WLAT * LEV * SLON
BLOCKS = ROWS // WLAT
SIDE = BLOCKS * HALF
PAY = SIDE + 16
EDGE = 40
LAT_RUN = 4
LON_RUN = 16
F32 = jnp.float32
BF16 = jnp.bfloat16
LIMIT = 24 * 1024 * 1024


def mm(a, b):
    return jnp.dot(a, b, preferred_element_type=F32)


def mm_nt(a, b):
    return lax.dot_general(a, b, (((1,), (1,)), ((), ())), preferred_element_type=F32)


def iota(shape, dim):
    return lax.broadcasted_iota(jnp.int32, shape, dim)


def place_of(n, odd_lat):
    l = jnp.where(n >= SIDE // 2, 1, 0)
    n = n - SIDE // 2 * l
    c = sum(jnp.where(n >= ROWS * q, 1, 0) for q in range(1, SLON))
    i = n - ROWS * c
    top = 3 * HALF + HALF // 2 * odd_lat + 12 * i
    bottom = 3 * HALF + HALF // 2 * (1 - odd_lat) + 12 * (i - (ROWS - SLAT))
    base = jnp.where(i < SLAT, top, jnp.where(i >= ROWS - SLAT, bottom, 12 * (i - SLAT)))
    return base + SLON * l + c, i, LEV * c + l


def layer_norm(x, gain, bias):
    center = x - jnp.mean(x, axis=-1, keepdims=True)
    spread = jnp.mean(center * center, axis=-1, keepdims=True)
    return (center * lax.rsqrt(spread + 1e-05) * gain + bias).astype(BF16)


def side_rows(s, l):
    odd = lax.axis_index("lon") % 2
    half = odd if s == 0 else 1 - odd
    return pl.multiple_of(l * SIDE + half * (SIDE // 2), SIDE // 2)


def prep_kernel(*refs):
    refs, (pay1, pay2, qlab, edge1, bend), weights, (lab, feat, ids, sem) = refs[:8], refs[8:13], refs[13:19], refs[19:]
    copies = [pltpu.make_async_copy(a, b, sem.at[i]) for i, (a, b) in enumerate(zip(refs, (feat, ids, *weights)))]
    for copy in copies:
        copy.start()
    odd_lon = lax.axis_index("lon") % 2
    odd_lat = lax.axis_index("lat") % 2
    first = lax.axis_index("lat") == 0
    place, lat, strip = place_of(iota((1, SIDE), 1), odd_lat)
    order = jnp.where(iota((SIDE, SIDE), 0) == place, 1.0, 0.0)
    spread = jnp.where(iota((128, SIDE), 0) == lat, 1.0, 0.0).astype(BF16)
    from_first = jnp.where((iota((LEV, ROWS), 1) < SLAT) & first, 4.0, 0.0)
    lab[...] = jnp.zeros_like(lab)
    row = iota((HALF, SIDE), 0)
    edge, edge_line = 0.0, 0.0
    for copy in copies[:2]:
        copy.wait()
    for s, pay in enumerate((pay1, pay2)):
        tokens = jnp.concatenate([feat[pl.ds(side_rows(s, l), SIDE // 2), :] for l in range(LEV)], axis=0)
        ordered = mm(order.astype(BF16), tokens)
        pay[:SIDE, :] = ordered.astype(BF16)
        half = odd_lon if s == 0 else 1 - odd_lon
        for c in range(SLON):
            lab[s, LEV * c : LEV * (c + 1), :ROWS] = ids[SLON * half + c].astype(F32) + from_first
        line = mm(lab[s].astype(BF16), spread)
        line = jnp.sum(jnp.where(iota((16, SIDE), 0) == strip, line, 0.0), axis=0, keepdims=True)
        qlab[s] = jnp.broadcast_to(jnp.sum(order * line, axis=-1, keepdims=True), (SIDE, 128))
        line = jnp.broadcast_to(line, (16, SIDE)).astype(BF16)
        ordered_line = jnp.concatenate([mm_nt(line, order.astype(BF16)), jnp.zeros((16, D - SIDE), F32)], axis=1)
        pay[SIDE:, :] = ordered_line.astype(BF16)
        wanted = jnp.where(row - HALF // 2 * s + 3 * HALF == place, 1.0, 0.0)
        wanted = jnp.where((row < HALF // 2) if s == 0 else (row >= HALF // 2), wanted, 0.0).astype(BF16)
        edge = edge + mm(wanted, tokens)
        edge_line = edge_line + mm_nt(line, wanted)
        if s == 0:
            moved = shifted(ordered_line[:8], 3 * HALF, 0)
            bend[...] = jnp.concatenate([ordered[3 * HALF : 3 * HALF + EDGE], moved], axis=0).astype(BF16)
    edge_line = jnp.concatenate([edge_line[:8], jnp.zeros((8, D - HALF), F32)], axis=1)
    edge1[...] = jnp.concatenate([edge, edge_line], axis=0).astype(BF16)
    for copy in copies[2:]:
        copy.wait()


def own_part(pay1, pay2, gain, bias, w_qkv, b_qkv, qkv, back, back_edge):
    g, b = gain[...].reshape(1, D), bias[...].reshape(1, D)
    for s, pay in enumerate((pay1, pay2)):
        normed = layer_norm(pay[:SIDE, :].astype(F32), g, b)
        for c in range(3):
            cols = slice(c * D, (c + 1) * D)
            part = mm(normed, w_qkv[:, cols]) + b_qkv[cols].reshape(1, D)
            part = part.astype(BF16).astype(F32)
            if c == 0:
                part = part * HS ** (-0.5)
            for m in range(BLOCKS):
                qkv[s, m, :, cols] = part[m * HALF : (m + 1) * HALF].astype(BF16)
    place, _, _ = place_of(iota((SIDE, 1), 0), lax.axis_index("lat") % 2)
    back[...] = jnp.where(iota((SIDE, 3 * HALF), 1) == place, 1.0, 0.0).astype(BF16)
    back_edge[...] = jnp.where(iota((SIDE, HALF), 1) + 3 * HALF == place, 1.0, 0.0).astype(BF16)


def turn():
    lat, lon = lax.axis_index("lat"), lax.axis_index("lon")
    early = (lat < LAT_RUN) & (lon % LON_RUN < 6)
    return jnp.where(early, jnp.where((lat == 0) & (lon == 0), 1, 0), 2)


def own_kernel(when, pay1, pay2, *refs):
    outs = refs[-4:-1] if when < 2 else refs[-3:]

    @pl.when(turn() == when)
    def _():
        own_part(pay1, pay2, *refs[:4], *outs)


def label_line(ref, at):
    return ref[...].astype(F32)[at : at + 8]


def shifted(line, start, to):
    return pltpu.roll(line, (to - start) % D, 1)


def attention(q, k, v, q_label, k_label):
    n = q.shape[0]
    keys = k.shape[0]
    wide = 4 * HS
    allowed = q_label == k_label
    out = []
    col = iota((1, wide), 1)
    for g in range(2):
        cols = slice(g * wide, (g + 1) * wide)
        own = [(col >= h * HS) & (col < (h + 1) * HS) for h in range(4)]
        qg = q[:, cols]
        stacked = jnp.concatenate([jnp.where(o, qg, 0.0) for o in own], axis=0).astype(BF16)
        scores = mm_nt(stacked, k[:, cols])
        scores = jnp.where(allowed[None], scores.reshape(4, n, keys), -1e30).reshape(4 * n, keys)
        expd = jnp.exp(scores - jnp.max(scores, axis=-1, keepdims=True))
        full = mm(expd.astype(BF16), v[:, cols])
        share = 1.0 / jnp.sum(expd, axis=-1, keepdims=True)
        picked = full[:n] * share[:n]
        for h in range(1, 4):
            rows = slice(h * n, (h + 1) * n)
            picked = jnp.where(own[h], full[rows] * share[rows], picked)
        out.append(picked)
    return jnp.concatenate(out, axis=1)


def finish(heads, x, w_out, b_out):
    projected = (mm(heads.astype(BF16), w_out) + b_out).astype(BF16).astype(F32)
    return (x + projected).astype(BF16)


def edge_piece(ref, e):
    at = 3 * HALF + 32 * e
    return ref[...].astype(F32)[at : at + EDGE]


def edge_labels(parts):
    lane = iota((8, D), 1)
    out = jnp.zeros((8, D), F32)
    for j, (line, start) in enumerate(parts):
        out = jnp.where((lane >= j * EDGE) & (lane < (j + 1) * EDGE), shifted(line, start, j * EDGE), out)
    return out


def corner_piece(ref):
    return jnp.concatenate([edge_piece(ref, 0), shifted(label_line(ref, SIDE), 3 * HALF, 0)], axis=0).astype(BF16)


def second_kernel(pay1, far1, pay2, far2, out):
    refs = (pay1, far1, pay2, far2)
    rows = [edge_piece(ref, 1) for ref in refs]
    line = edge_labels([(label_line(ref, SIDE), 3 * HALF + 32) for ref in refs])
    out[...] = jnp.concatenate([*rows, line, line], axis=0).astype(BF16)


def bend_kernel(far1, after, out):
    del after
    out[...] = corner_piece(far1)


def third_kernel(over, crossed, after, out):
    del after
    x = over_first(over, crossed)
    out[...] = jnp.concatenate([x[32 : 32 + EDGE], shifted(x[HALF:], 32, 0)], axis=0).astype(BF16)


def is_far(axis, run):
    at = lax.axis_index(axis) % run
    return (at == 0) | (at == run - 1)


def choose(flag, a, b):
    return jnp.where(jnp.full(a.shape, jnp.where(flag, 1.0, 0.0)) > 0.5, a, b)


def over_first(over, crossed):
    crosses = is_far("lat", LAT_RUN) & jnp.logical_not(is_far("lon", LON_RUN))
    return choose(crosses, crossed[...].astype(F32), over[...].astype(F32))


def gate_kernel(x, after, out):
    del after
    out[...] = x[...]


def inner_kernel(pay1, pay2, far1, far2, qlab, qkv, back, gain, bias, w_qkv, b_qkv, w_out, b_out, kv_edge, placed, kv):
    g, b = gain[...].reshape(1, D), bias[...].reshape(1, D)
    for s, far in enumerate((far1, far2)):
        normed = layer_norm(far[:SIDE, :].astype(F32), g, b)
        for c in range(2):
            cols = slice((c + 1) * D, (c + 2) * D)
            part = mm(normed, w_qkv[:, cols]) + b_qkv[cols].reshape(1, D)
            kv[s, :, c * D : (c + 1) * D] = part
            kv_edge[s, :, c * D : (c + 1) * D] = part[3 * HALF :].astype(BF16)
    mixed = ([], [])
    for m in range(BLOCKS - 1):
        rows = slice(m * HALF, (m + 1) * HALF)
        heads, xs = [], []
        for s, (pay, far) in enumerate(((pay1, far1), (pay2, far2))):
            both = jnp.concatenate([qkv[s, m, :, D:].astype(F32), kv[s, rows, :]], axis=0).astype(BF16)
            own_line = shifted(label_line(pay, SIDE), m * HALF, 0)[:1, : 2 * HALF]
            far_line = shifted(label_line(far, SIDE), m * HALF, HALF)[:1, : 2 * HALF]
            k_label = jnp.where(iota((1, 2 * HALF), 1) < HALF, own_line, far_line)
            q_label = qlab[s, rows, :][:, :1]
            heads.append(attention(qkv[s, m, :, :D].astype(F32), both[:, :D], both[:, D:], q_label, k_label))
            xs.append(pay[:SIDE, :].astype(F32)[rows])
        done = finish(jnp.concatenate(heads, axis=0), jnp.concatenate(xs, axis=0), w_out[...], b_out[...].reshape(1, D))
        done = done.astype(F32)
        mixed[0].append(done[:HALF])
        mixed[1].append(done[HALF:])
    for s in range(2):
        placed[s] = mm(back[...], jnp.concatenate(mixed[s], axis=0).astype(BF16)).astype(BF16)


def project_kv(x, g, b, w_qkv, b_qkv):
    normed = layer_norm(x, g, b)
    return [
        mm(normed, w_qkv[:, (c + 1) * D : (c + 2) * D]) + b_qkv[(c + 1) * D : (c + 2) * D].reshape(1, D) for c in range(2)
    ]


def edge_window(e, s, pay, far, over_kv, over_line, late, qlab, qkv, kv_edge):
    last = BLOCKS - 1
    keys = []
    for c in range(2):
        own = qkv[s, last, :, (c + 1) * D : (c + 2) * D].astype(F32)
        far_part = kv_edge[s, :, c * D : (c + 1) * D].astype(F32)
        keys.append(jnp.concatenate([own, far_part, over_kv[c]], axis=0).astype(BF16))
    count = 2 * HALF + 2 * EDGE
    lane = iota((1, count), 1)
    own_line = shifted(label_line(pay, SIDE), last * HALF, 0)[:1, :count]
    far_line = shifted(label_line(far, SIDE), last * HALF, HALF)[:1, :count]
    k_label = jnp.where(lane < HALF, own_line, jnp.where(lane < 2 * HALF, far_line, over_line[:1, :count]))
    piece = lane - 2 * HALF
    piece = jnp.where(piece >= EDGE, piece - EDGE, piece)
    spot = jnp.where(lane < HALF, lane, jnp.where(lane < 2 * HALF, lane - HALF, piece))
    from_row = jnp.where(lane < 2 * HALF, HALF // 2 * e, EDGE - HALF // 2 if late else 0)
    mine = (spot >= from_row) & (spot < from_row + HALF // 2)
    k_label = jnp.where(mine, k_label, -1.0)
    at = 32 * e
    q = qkv[s, last, :, :D].astype(F32)[at : at + EDGE]
    q_label = qlab[s, last * HALF : SIDE, :][at : at + EDGE, :1]
    return attention(q, keys[0], keys[1], q_label, k_label)


def near_kernel(when, pay1, pay2, far1, far2, over2, qlab, qkv, kv_edge, gain, bias, w_qkv, b_qkv, *refs):
    out = refs[-1]
    crosses = is_far("lat", LAT_RUN) & jnp.logical_not(is_far("lon", LON_RUN))

    @pl.when(jnp.logical_not(crosses) if when else crosses)
    def _():
        g, b = gain[...].reshape(1, D), bias[...].reshape(1, D)
        kv = project_kv(over2[...].astype(F32), g, b, w_qkv, b_qkv)
        line = label_line(over2, 4 * EDGE)
        for s, (pay, far) in enumerate(((pay1, far1), (pay2, far2))):
            part = [k[2 * EDGE * s : 2 * EDGE * (s + 1)] for k in kv]
            out[s] = edge_window(1, s, pay, far, part, shifted(line, 2 * EDGE * s, 2 * HALF), True, qlab, qkv, kv_edge)


def outer_kernel(
    pay1, pay2, far1, far2, over, crossed, bend1, bend2, bend4, near, qlab, qkv, kv_edge, placed, back, gain, bias, w_qkv, b_qkv, w_out, b_out, out, done, sem
):
    g, b = gain[...].reshape(1, D), bias[...].reshape(1, D)
    over1 = over_first(over, crossed)
    corner, raw = bend1[...].astype(F32) + bend2[...].astype(F32), over[...].astype(F32)
    crosses = is_far("lat", LAT_RUN) & jnp.logical_not(is_far("lon", LON_RUN))
    corner = choose(crosses, jnp.concatenate([raw[:EDGE], raw[HALF:]], axis=0), corner)
    other = bend4[...].astype(F32)
    kv = project_kv(jnp.concatenate([over1, corner, other], axis=0), g, b, w_qkv, b_qkv)
    line = over1[HALF:]
    lane = iota((8, D), 1)
    rest = (qlab, qkv, kv_edge)
    a = []
    for s, (pay, far, bent) in enumerate(((pay1, far1, corner), (pay2, far2, other))):
        at = over1.shape[0] + (EDGE + 8) * s
        kv_s = [jnp.concatenate([k[32 * s : 32 * s + EDGE], k[at : at + EDGE]], axis=0) for k in kv]
        mine, theirs = shifted(line, 32 * s, 2 * HALF), shifted(bent[EDGE:], 0, 2 * HALF + EDGE)
        line_s = jnp.where(lane < 2 * HALF + EDGE, mine, theirs)
        a.append(edge_window(0, s, pay, far, kv_s, line_s, s == 1, *rest))
    heads, xs = [], []
    for s, pay in enumerate((pay1, pay2)):
        z = near[s]
        mid = jnp.where(iota((8, 1), 0) < 4, a[s][32:], z[:8])
        heads.append(jnp.concatenate([a[s][:32], mid, z[8:]], axis=0))
        xs.append(pay[:SIDE, :].astype(F32)[3 * HALF :])
    edges = finish(jnp.concatenate(heads, axis=0), jnp.concatenate(xs, axis=0), w_out[...], b_out[...].reshape(1, D))
    copies = []
    for s in range(2):
        for l in range(LEV):
            rows = pl.ds(l * (SIDE // 2), SIDE // 2)
            product = mm(back[rows, :], edges[s * HALF : (s + 1) * HALF])
            done[s, rows, :] = (product + placed[s, rows, :].astype(F32)).astype(BF16)
            copies.append(
                pltpu.make_async_copy(done.at[s, rows], out.at[pl.ds(side_rows(s, l), SIDE // 2)], sem.at[2 * s + l])
            )
            copies[-1].start()
    for copy in copies:
        copy.wait()


VMEM = pl.BlockSpec(memory_space=pltpu.VMEM)


def cost(flops, moved, exps=0):
    return pl.CostEstimate(flops=flops, bytes_accessed=moved, transcendentals=exps)


def call(kernel, name, outs, args, flops, scratch=(), keep=True, spec=VMEM, aliases=()):
    make = pltpu.VMEM if keep else jax.ShapeDtypeStruct
    return pl.pallas_call(
        kernel,
        out_shape=[make(shape, dtype) for shape, dtype in outs],
        in_specs=[spec] * len(args),
        out_specs=[VMEM if keep else pl.BlockSpec(memory_space=pl.ANY)] * len(outs),
        scratch_shapes=list(scratch),
        input_output_aliases=dict(aliases),
        compiler_params=pltpu.CompilerParams(vmem_limit_bytes=LIMIT),
        cost_estimate=cost(flops, 4_000_000, 500_000),
        name=name,
    )(*args)


def held(x):
    return pltpu.with_memory_space_constraint(x, pltpu.VMEM)


def gate(x, after):
    return held(call(gate_kernel, "gate", [(x.shape, x.dtype)], (held(x), after), 1_000)[0])


def pairs(axis, first):
    n = lax.axis_size(axis)
    return [(i, (i + 1) % n) for i in range(first, n, 2)]


def swap(block, axis, first):
    route = [way for i, j in pairs(axis, first) for way in ((i, j), (j, i))]
    return held(lax.ppermute(block, axis, route))


def swap_far(block, way):
    n_lon, n_lat = lax.axis_size("lon"), lax.axis_size("lat")
    over_lon = {i: j for p in pairs("lon", 1) for i, j in (p, p[::-1])}
    over_lat = {i: j for p in pairs("lat", 1) for i, j in (p, p[::-1])}
    route = []
    for o in range(n_lon):
        for a in range(n_lat):
            far_lat = a % LAT_RUN in (0, LAT_RUN - 1)
            far_lon = o % LON_RUN in (0, LON_RUN - 1)
            own = "direct" if far_lat and far_lon else "lon" if far_lat else "lat"
            if way in (own, "first"):
                to_o = over_lon[o] if own == "lon" or way == "direct" else o
                to_a = a if way == "lon" else over_lat[a]
                route.append((o * n_lat + a, to_o * n_lat + to_a))
    return held(lax.ppermute(block, ("lon", "lat"), route))


def local(features, region_ids, ln_gain, ln_bias, w_qkv, b_qkv, w_out, b_out):
    feat = features.transpose(0, 2, 1, 3).reshape(2 * SIDE, D)
    ids = region_ids.transpose(2, 0, 1)
    weights = (ln_gain, ln_bias, w_qkv, b_qkv, w_out, b_out)
    pay1, pay2, qlab, edge1, bend, *weights = call(
        prep_kernel,
        "prep",
        [
            *[((PAY, D), BF16), ((PAY, D), BF16), ((2, SIDE, 128), F32), ((HALF + 8, D), BF16), ((EDGE + 8, D), BF16)],
            *[(w.shape, w.dtype) for w in weights],
        ],
        [pltpu.with_memory_space_constraint(x, pltpu.HBM) for x in (feat, ids, *weights)],
        200_000_000,
        [
            pltpu.VMEM((2, 16, 128), F32),
            pltpu.VMEM(feat.shape, BF16),
            pltpu.VMEM(ids.shape, jnp.int32),
            pltpu.SemaphoreType.DMA((8,)),
        ],
        spec=pl.BlockSpec(memory_space=pl.ANY),
    )
    weights = [held(w) for w in weights]
    norm, into, outof = weights[:2], weights[2:4], weights[4:]
    parts = [((2, BLOCKS, HALF, 3 * D), BF16), ((SIDE, 3 * HALF), BF16), ((SIDE, HALF), BF16)]

    def own(when, more, aliases):
        name = ("at_once", "after", "late")[when]
        args = (held(pay1), held(pay2), *norm, *into, *more)
        outs = parts + ([((PAY, D), BF16)] if when < 2 else [])
        results = call(functools.partial(own_kernel, when), name, outs, args, 900_000_000, aliases=aliases)
        return [held(x) for x in results[:3]], *results[3:]

    ours, pay2 = own(0, (), {1: 3})
    pay2 = held(pay2)
    far2 = swap(pay2, "lon", 0)
    ours, pay1 = own(1, ours, {0: 3, 6: 0, 7: 1, 8: 2})
    pay1, qlab = held(pay1), held(qlab)
    far1 = swap(pay1, "lon", 1)
    edge1 = gate(edge1, far2)
    over = swap_far(edge1, "first")
    bend = gate(bend, edge1)
    bend1 = swap_far(bend, "direct")
    ((qkv, back, back_edge),) = own(2, (*ours, far1), {6: 0, 7: 1, 8: 2})
    (edge2,) = call(second_kernel, "edge2", [((4 * EDGE + 16, D), BF16)], (pay1, far1, pay2, far2), 1_000_000)
    over2 = swap(edge2, "lat", 0)
    (bend,) = call(bend_kernel, "bend", [((EDGE + 8, D), BF16)], (far1, held(bend)), 1_000_000)
    bend2 = swap_far(bend, "lat")
    kv_edge, placed = call(
        inner_kernel,
        "inner",
        [((2, HALF, 2 * D), BF16), ((2, SIDE, D), BF16)],
        (pay1, pay2, far1, far2, qlab, qkv, back, *norm, *into, *outof),
        3_000_000_000,
        [pltpu.VMEM((2, SIDE, 2 * D), F32)],
    )
    kv_edge, placed = held(kv_edge), held(placed)
    raw = gate(over, kv_edge)
    crossed = swap_far(raw, "lon")

    def near(when, *more):
        args = (pay1, pay2, far1, far2, over2, qlab, qkv, kv_edge, *norm, *into, *more)
        kernel, aliases = functools.partial(near_kernel, when), {13: 0} if when else {}
        return held(call(kernel, "near", [((2, EDGE, D), F32)], args, 1_000_000_000, aliases=aliases)[0])

    windows = near(0, raw)
    (bend,) = call(third_kernel, "third", [((EDGE + 8, D), BF16)], (raw, crossed, windows), 1_000_000)
    bend4 = swap(bend, "lon", 0)
    windows = near(1, held(bend), windows)
    (out,) = call(
        outer_kernel,
        "outer",
        [((2 * SIDE, D), BF16)],
        (
            *(pay1, pay2, far1, far2, raw, crossed, bend1, bend2, bend4, windows),
            *(qlab, qkv, kv_edge, placed, back_edge, *norm, *into, *outof),
        ),
        1_500_000_000,
        [pltpu.VMEM((2, SIDE, D), BF16), pltpu.SemaphoreType.DMA((4,))],
        keep=False,
    )
    return out.reshape(LEV, COLS, ROWS, D).transpose(0, 2, 1, 3)


def solution(mesh):
    return jax.shard_map(
        local,
        mesh=mesh,
        in_specs=(P(None, "lat", "lon", None), P(None, "lat", "lon"), P(), P(), P(), P(), P(), P()),
        out_specs=P(None, "lat", "lon", None),
        check_vma=False,
    )
```

```python
import functools

import jax
import jax.numpy as jnp
from jax import lax
from jax.experimental import pallas as pl
from jax.experimental.pallas import tpu as pltpu
from jax.sharding import PartitionSpec as P

HEADS = 8
WLAT = 6
WLON = 12
SLAT = 3
SLON = 6
LEV = 2
D = 512
HS = D // HEADS
ROWS = 24
COLS = 12
HALF = WLAT * LEV * SLON
BLOCKS = ROWS // WLAT
SIDE = BLOCKS * HALF
PAY = SIDE + 16
EDGE = 40
LAT_RUN = 4
LON_RUN = 16
F32 = jnp.float32
BF16 = jnp.bfloat16
LIMIT = 24 * 1024 * 1024


def mm(a, b):
    return jnp.dot(a, b, preferred_element_type=F32)


def mm_nt(a, b):
    return lax.dot_general(a, b, (((1,), (1,)), ((), ())), preferred_element_type=F32)


def iota(shape, dim):
    return lax.broadcasted_iota(jnp.int32, shape, dim)


def place_of(n, odd_lat):
    l = jnp.where(n >= SIDE // 2, 1, 0)
    n = n - SIDE // 2 * l
    c = sum(jnp.where(n >= ROWS * q, 1, 0) for q in range(1, SLON))
    i = n - ROWS * c
    top = 3 * HALF + HALF // 2 * odd_lat + 12 * i
    bottom = 3 * HALF + HALF // 2 * (1 - odd_lat) + 12 * (i - (ROWS - SLAT))
    base = jnp.where(i < SLAT, top, jnp.where(i >= ROWS - SLAT, bottom, 12 * (i - SLAT)))
    return base + SLON * l + c, i, LEV * c + l


def layer_norm(x, gain, bias):
    center = x - jnp.mean(x, axis=-1, keepdims=True)
    spread = jnp.mean(center * center, axis=-1, keepdims=True)
    return (center * lax.rsqrt(spread + 1e-05) * gain + bias).astype(BF16)


def side_rows(s, l):
    odd = lax.axis_index("lon") % 2
    half = odd if s == 0 else 1 - odd
    return pl.multiple_of(l * SIDE + half * (SIDE // 2), SIDE // 2)


def prep_kernel(*refs):
    refs, (pay1, pay2, qlab, edge1, bend), weights, (lab, feat, ids, sem) = refs[:8], refs[8:13], refs[13:19], refs[19:]
    copies = [pltpu.make_async_copy(a, b, sem.at[i]) for i, (a, b) in enumerate(zip(refs, (feat, ids, *weights)))]
    for copy in copies:
        copy.start()
    odd_lon = lax.axis_index("lon") % 2
    odd_lat = lax.axis_index("lat") % 2
    first = lax.axis_index("lat") == 0
    place, lat, strip = place_of(iota((1, SIDE), 1), odd_lat)
    order = jnp.where(iota((SIDE, SIDE), 0) == place, 1.0, 0.0)
    spread = jnp.where(iota((128, SIDE), 0) == lat, 1.0, 0.0).astype(BF16)
    from_first = jnp.where((iota((LEV, ROWS), 1) < SLAT) & first, 4.0, 0.0)
    lab[...] = jnp.zeros_like(lab)
    row = iota((HALF, SIDE), 0)
    edge, edge_line = 0.0, 0.0
    for copy in copies[:2]:
        copy.wait()
    for s, pay in enumerate((pay1, pay2)):
        tokens = jnp.concatenate([feat[pl.ds(side_rows(s, l), SIDE // 2), :] for l in range(LEV)], axis=0)
        ordered = mm(order.astype(BF16), tokens)
        pay[:SIDE, :] = ordered.astype(BF16)
        half = odd_lon if s == 0 else 1 - odd_lon
        for c in range(SLON):
            lab[s, LEV * c : LEV * (c + 1), :ROWS] = ids[SLON * half + c].astype(F32) + from_first
        line = mm(lab[s].astype(BF16), spread)
        line = jnp.sum(jnp.where(iota((16, SIDE), 0) == strip, line, 0.0), axis=0, keepdims=True)
        qlab[s] = jnp.broadcast_to(jnp.sum(order * line, axis=-1, keepdims=True), (SIDE, 128))
        line = jnp.broadcast_to(line, (16, SIDE)).astype(BF16)
        ordered_line = jnp.concatenate([mm_nt(line, order.astype(BF16)), jnp.zeros((16, D - SIDE), F32)], axis=1)
        pay[SIDE:, :] = ordered_line.astype(BF16)
        wanted = jnp.where(row - HALF // 2 * s + 3 * HALF == place, 1.0, 0.0)
        wanted = jnp.where((row < HALF // 2) if s == 0 else (row >= HALF // 2), wanted, 0.0).astype(BF16)
        edge = edge + mm(wanted, tokens)
        edge_line = edge_line + mm_nt(line, wanted)
        if s == 0:
            moved = shifted(ordered_line[:8], 3 * HALF, 0)
            bend[...] = jnp.concatenate([ordered[3 * HALF : 3 * HALF + EDGE], moved], axis=0).astype(BF16)
    edge_line = jnp.concatenate([edge_line[:8], jnp.zeros((8, D - HALF), F32)], axis=1)
    edge1[...] = jnp.concatenate([edge, edge_line], axis=0).astype(BF16)
    for copy in copies[2:]:
        copy.wait()


def own_part(pay1, pay2, gain, bias, w_qkv, b_qkv, qkv, back, back_edge):
    g, b = gain[...].reshape(1, D), bias[...].reshape(1, D)
    for s, pay in enumerate((pay1, pay2)):
        normed = layer_norm(pay[:SIDE, :].astype(F32), g, b)
        for c in range(3):
            cols = slice(c * D, (c + 1) * D)
            part = mm(normed, w_qkv[:, cols]) + b_qkv[cols].reshape(1, D)
            part = part.astype(BF16).astype(F32)
            if c == 0:
                part = part * HS ** (-0.5)
            for m in range(BLOCKS):
                qkv[s, m, :, cols] = part[m * HALF : (m + 1) * HALF].astype(BF16)
    place, _, _ = place_of(iota((SIDE, 1), 0), lax.axis_index("lat") % 2)
    back[...] = jnp.where(iota((SIDE, 3 * HALF), 1) == place, 1.0, 0.0).astype(BF16)
    back_edge[...] = jnp.where(iota((SIDE, HALF), 1) + 3 * HALF == place, 1.0, 0.0).astype(BF16)


def turn():
    lat, lon = lax.axis_index("lat"), lax.axis_index("lon")
    early = (lat < LAT_RUN) & (lon % LON_RUN < 6)
    return jnp.where(early, jnp.where((lat == 0) & (lon == 0), 1, 0), 2)


def own_kernel(when, pay1, pay2, *refs):
    outs = refs[-4:-1] if when < 2 else refs[-3:]

    @pl.when(turn() == when)
    def _():
        own_part(pay1, pay2, *refs[:4], *outs)


def label_line(ref, at):
    return ref[...].astype(F32)[at : at + 8]


def shifted(line, start, to):
    return pltpu.roll(line, (to - start) % D, 1)


def attention(q, k, v, q_label, k_label):
    n = q.shape[0]
    keys = k.shape[0]
    wide = 4 * HS
    allowed = q_label == k_label
    out = []
    col = iota((1, wide), 1)
    for g in range(2):
        cols = slice(g * wide, (g + 1) * wide)
        own = [(col >= h * HS) & (col < (h + 1) * HS) for h in range(4)]
        qg = q[:, cols]
        stacked = jnp.concatenate([jnp.where(o, qg, 0.0) for o in own], axis=0).astype(BF16)
        scores = mm_nt(stacked, k[:, cols])
        scores = jnp.where(allowed[None], scores.reshape(4, n, keys), -1e30).reshape(4 * n, keys)
        expd = jnp.exp(scores - jnp.max(scores, axis=-1, keepdims=True))
        full = mm(expd.astype(BF16), v[:, cols])
        share = 1.0 / jnp.sum(expd, axis=-1, keepdims=True)
        picked = full[:n] * share[:n]
        for h in range(1, 4):
            rows = slice(h * n, (h + 1) * n)
            picked = jnp.where(own[h], full[rows] * share[rows], picked)
        out.append(picked)
    return jnp.concatenate(out, axis=1)


def finish(heads, x, w_out, b_out):
    projected = (mm(heads.astype(BF16), w_out) + b_out).astype(BF16).astype(F32)
    return (x + projected).astype(BF16)


def edge_piece(ref, e):
    at = 3 * HALF + 32 * e
    return ref[...].astype(F32)[at : at + EDGE]


def edge_labels(parts):
    lane = iota((8, D), 1)
    out = jnp.zeros((8, D), F32)
    for j, (line, start) in enumerate(parts):
        out = jnp.where((lane >= j * EDGE) & (lane < (j + 1) * EDGE), shifted(line, start, j * EDGE), out)
    return out


def corner_piece(ref):
    return jnp.concatenate([edge_piece(ref, 0), shifted(label_line(ref, SIDE), 3 * HALF, 0)], axis=0).astype(BF16)


def second_kernel(pay1, far1, pay2, far2, out, bend):
    refs = (pay1, far1, pay2, far2)
    rows = [edge_piece(ref, 1) for ref in refs]
    line = edge_labels([(label_line(ref, SIDE), 3 * HALF + 32) for ref in refs])
    out[...] = jnp.concatenate([*rows, line, line], axis=0).astype(BF16)
    bend[...] = corner_piece(far1)


def gate_kernel(x, after, out):
    del after
    out[...] = x[...]


def third_kernel(over1, after, first, second):
    del after
    x, line = over1[...].astype(F32), label_line(over1, HALF)
    for out, at in ((first, 0), (second, 32)):
        out[...] = jnp.concatenate([x[at : at + EDGE], shifted(line, at, 0)], axis=0).astype(BF16)


def inner_kernel(pay1, pay2, far1, far2, qlab, qkv, back, gain, bias, w_qkv, b_qkv, w_out, b_out, kv_edge, placed, kv):
    g, b = gain[...].reshape(1, D), bias[...].reshape(1, D)
    for s, far in enumerate((far1, far2)):
        normed = layer_norm(far[:SIDE, :].astype(F32), g, b)
        for c in range(2):
            cols = slice((c + 1) * D, (c + 2) * D)
            part = mm(normed, w_qkv[:, cols]) + b_qkv[cols].reshape(1, D)
            kv[s, :, c * D : (c + 1) * D] = part
            kv_edge[s, :, c * D : (c + 1) * D] = part[3 * HALF :].astype(BF16)
    mixed = ([], [])
    for m in range(BLOCKS - 1):
        rows = slice(m * HALF, (m + 1) * HALF)
        heads, xs = [], []
        for s, (pay, far) in enumerate(((pay1, far1), (pay2, far2))):
            both = jnp.concatenate([qkv[s, m, :, D:].astype(F32), kv[s, rows, :]], axis=0).astype(BF16)
            own_line = shifted(label_line(pay, SIDE), m * HALF, 0)[:1, : 2 * HALF]
            far_line = shifted(label_line(far, SIDE), m * HALF, HALF)[:1, : 2 * HALF]
            k_label = jnp.where(iota((1, 2 * HALF), 1) < HALF, own_line, far_line)
            q_label = qlab[s, rows, :][:, :1]
            heads.append(attention(qkv[s, m, :, :D].astype(F32), both[:, :D], both[:, D:], q_label, k_label))
            xs.append(pay[:SIDE, :].astype(F32)[rows])
        done = finish(jnp.concatenate(heads, axis=0), jnp.concatenate(xs, axis=0), w_out[...], b_out[...].reshape(1, D))
        done = done.astype(F32)
        mixed[0].append(done[:HALF])
        mixed[1].append(done[HALF:])
    for s in range(2):
        placed[s] = mm(back[...], jnp.concatenate(mixed[s], axis=0).astype(BF16)).astype(BF16)


def project_kv(x, g, b, w_qkv, b_qkv):
    normed = layer_norm(x, g, b)
    return [
        mm(normed, w_qkv[:, (c + 1) * D : (c + 2) * D]) + b_qkv[(c + 1) * D : (c + 2) * D].reshape(1, D) for c in range(2)
    ]


def edge_window(e, s, pay, far, over_kv, over_line, late, qlab, qkv, kv_edge):
    last = BLOCKS - 1
    keys = []
    for c in range(2):
        own = qkv[s, last, :, (c + 1) * D : (c + 2) * D].astype(F32)
        far_part = kv_edge[s, :, c * D : (c + 1) * D].astype(F32)
        keys.append(jnp.concatenate([own, far_part, over_kv[c]], axis=0).astype(BF16))
    count = 2 * HALF + 2 * EDGE
    lane = iota((1, count), 1)
    own_line = shifted(label_line(pay, SIDE), last * HALF, 0)[:1, :count]
    far_line = shifted(label_line(far, SIDE), last * HALF, HALF)[:1, :count]
    k_label = jnp.where(lane < HALF, own_line, jnp.where(lane < 2 * HALF, far_line, over_line[:1, :count]))
    piece = lane - 2 * HALF
    piece = jnp.where(piece >= EDGE, piece - EDGE, piece)
    spot = jnp.where(lane < HALF, lane, jnp.where(lane < 2 * HALF, lane - HALF, piece))
    from_row = jnp.where(lane < 2 * HALF, HALF // 2 * e, EDGE - HALF // 2 if late else 0)
    mine = (spot >= from_row) & (spot < from_row + HALF // 2)
    k_label = jnp.where(mine, k_label, -1.0)
    at = 32 * e
    q = qkv[s, last, :, :D].astype(F32)[at : at + EDGE]
    q_label = qlab[s, last * HALF : SIDE, :][at : at + EDGE, :1]
    return attention(q, keys[0], keys[1], q_label, k_label)


def near_kernel(pay1, pay2, far1, far2, over2, qlab, qkv, kv_edge, gain, bias, w_qkv, b_qkv, out):
    g, b = gain[...].reshape(1, D), bias[...].reshape(1, D)
    kv = project_kv(over2[...].astype(F32), g, b, w_qkv, b_qkv)
    line = label_line(over2, 4 * EDGE)
    for s, (pay, far) in enumerate(((pay1, far1), (pay2, far2))):
        part = [k[2 * EDGE * s : 2 * EDGE * (s + 1)] for k in kv]
        out[s] = edge_window(1, s, pay, far, part, shifted(line, 2 * EDGE * s, 2 * HALF), True, qlab, qkv, kv_edge)


def outer_kernel(
    pay1, pay2, far1, far2, over1, bend1, bend2, bend3, bend4, near, qlab, qkv, kv_edge, placed, back, gain, bias, w_qkv, b_qkv, w_out, b_out, out, done, sem
):
    g, b = gain[...].reshape(1, D), bias[...].reshape(1, D)
    corner = bend1[...].astype(F32) + bend2[...].astype(F32) + bend3[...].astype(F32)
    other = bend4[...].astype(F32)
    kv = project_kv(jnp.concatenate([over1[...].astype(F32), corner, other], axis=0), g, b, w_qkv, b_qkv)
    line = label_line(over1, HALF)
    lane = iota((8, D), 1)
    rest = (qlab, qkv, kv_edge)
    a = []
    for s, (pay, far, bent) in enumerate(((pay1, far1, corner), (pay2, far2, other))):
        at = over1.shape[0] + (EDGE + 8) * s
        kv_s = [jnp.concatenate([k[32 * s : 32 * s + EDGE], k[at : at + EDGE]], axis=0) for k in kv]
        mine, theirs = shifted(line, 32 * s, 2 * HALF), shifted(bent[EDGE:], 0, 2 * HALF + EDGE)
        line_s = jnp.where(lane < 2 * HALF + EDGE, mine, theirs)
        a.append(edge_window(0, s, pay, far, kv_s, line_s, s == 1, *rest))
    heads, xs = [], []
    for s, pay in enumerate((pay1, pay2)):
        z = near[s]
        mid = jnp.where(iota((8, 1), 0) < 4, a[s][32:], z[:8])
        heads.append(jnp.concatenate([a[s][:32], mid, z[8:]], axis=0))
        xs.append(pay[:SIDE, :].astype(F32)[3 * HALF :])
    edges = finish(jnp.concatenate(heads, axis=0), jnp.concatenate(xs, axis=0), w_out[...], b_out[...].reshape(1, D))
    copies = []
    for s in range(2):
        for l in range(LEV):
            rows = pl.ds(l * (SIDE // 2), SIDE // 2)
            product = mm(back[rows, :], edges[s * HALF : (s + 1) * HALF])
            done[s, rows, :] = (product + placed[s, rows, :].astype(F32)).astype(BF16)
            copies.append(
                pltpu.make_async_copy(done.at[s, rows], out.at[pl.ds(side_rows(s, l), SIDE // 2)], sem.at[2 * s + l])
            )
            copies[-1].start()
    for copy in copies:
        copy.wait()


VMEM = pl.BlockSpec(memory_space=pltpu.VMEM)


def cost(flops, moved, exps=0):
    return pl.CostEstimate(flops=flops, bytes_accessed=moved, transcendentals=exps)


def call(kernel, name, outs, args, flops, scratch=(), keep=True, spec=VMEM, aliases=()):
    make = pltpu.VMEM if keep else jax.ShapeDtypeStruct
    return pl.pallas_call(
        kernel,
        out_shape=[make(shape, dtype) for shape, dtype in outs],
        in_specs=[spec] * len(args),
        out_specs=[VMEM if keep else pl.BlockSpec(memory_space=pl.ANY)] * len(outs),
        scratch_shapes=list(scratch),
        input_output_aliases=dict(aliases),
        compiler_params=pltpu.CompilerParams(vmem_limit_bytes=LIMIT),
        cost_estimate=cost(flops, 4_000_000, 500_000),
        name=name,
    )(*args)


def held(x):
    return pltpu.with_memory_space_constraint(x, pltpu.VMEM)


def gate(x, after):
    return held(call(gate_kernel, "gate", [(x.shape, x.dtype)], (held(x), after), 1_000)[0])


def pairs(axis, first):
    n = lax.axis_size(axis)
    return [(i, (i + 1) % n) for i in range(first, n, 2)]


def swap(block, axis, first):
    route = [way for i, j in pairs(axis, first) for way in ((i, j), (j, i))]
    return held(lax.ppermute(block, axis, route))


def swap_corners(block, way):
    n_lon, n_lat = lax.axis_size("lon"), lax.axis_size("lat")
    over_lon = {i: j for p in pairs("lon", 1) for i, j in (p, p[::-1])}
    over_lat = {i: j for p in pairs("lat", 1) for i, j in (p, p[::-1])}
    route = []
    for o in range(n_lon):
        for a in range(n_lat):
            far_lat = a % LAT_RUN in (0, LAT_RUN - 1)
            far_lon = o % LON_RUN in (0, LON_RUN - 1)
            if way == ("direct" if far_lat and far_lon else "lon" if far_lat else "lat"):
                to = (o if way == "lat" else over_lon[o]) * n_lat + (a if way == "lon" else over_lat[a])
                route.append((o * n_lat + a, to))
    return held(lax.ppermute(block, ("lon", "lat"), route))


def local(features, region_ids, ln_gain, ln_bias, w_qkv, b_qkv, w_out, b_out):
    feat = features.transpose(0, 2, 1, 3).reshape(2 * SIDE, D)
    ids = region_ids.transpose(2, 0, 1)
    weights = (ln_gain, ln_bias, w_qkv, b_qkv, w_out, b_out)
    pay1, pay2, qlab, edge1, bend, *weights = call(
        prep_kernel,
        "prep",
        [
            *[((PAY, D), BF16), ((PAY, D), BF16), ((2, SIDE, 128), F32), ((HALF + 8, D), BF16), ((EDGE + 8, D), BF16)],
            *[(w.shape, w.dtype) for w in weights],
        ],
        [pltpu.with_memory_space_constraint(x, pltpu.HBM) for x in (feat, ids, *weights)],
        200_000_000,
        [
            pltpu.VMEM((2, 16, 128), F32),
            pltpu.VMEM(feat.shape, BF16),
            pltpu.VMEM(ids.shape, jnp.int32),
            pltpu.SemaphoreType.DMA((8,)),
        ],
        spec=pl.BlockSpec(memory_space=pl.ANY),
    )
    weights = [held(w) for w in weights]
    norm, into, outof = weights[:2], weights[2:4], weights[4:]
    parts = [((2, BLOCKS, HALF, 3 * D), BF16), ((SIDE, 3 * HALF), BF16), ((SIDE, HALF), BF16)]

    def own(when, more, aliases):
        name = ("at_once", "after", "late")[when]
        args = (held(pay1), held(pay2), *norm, *into, *more)
        outs = parts + ([((PAY, D), BF16)] if when < 2 else [])
        results = call(functools.partial(own_kernel, when), name, outs, args, 900_000_000, aliases=aliases)
        return [held(x) for x in results[:3]], *results[3:]

    ours, pay2 = own(0, (), {1: 3})
    pay2 = held(pay2)
    far2 = swap(pay2, "lon", 0)
    ours, pay1 = own(1, ours, {0: 3, 6: 0, 7: 1, 8: 2})
    pay1, qlab = held(pay1), held(qlab)
    far1 = swap(pay1, "lon", 1)
    edge1 = gate(edge1, far2)
    over1 = swap(edge1, "lat", 1)
    bend = gate(bend, edge1)
    bend1 = swap_corners(bend, "direct")
    ((qkv, back, back_edge),) = own(2, (*ours, far1), {6: 0, 7: 1, 8: 2})
    edge2, bend = call(
        second_kernel,
        "edge2",
        [((4 * EDGE + 16, D), BF16), ((EDGE + 8, D), BF16)],
        (pay1, far1, pay2, far2),
        1_000_000,
    )
    bend2 = swap_corners(bend, "lat")
    over2 = swap(edge2, "lat", 0)
    kv_edge, placed = call(
        inner_kernel,
        "inner",
        [((2, HALF, 2 * D), BF16), ((2, SIDE, D), BF16)],
        (pay1, pay2, far1, far2, qlab, qkv, back, *norm, *into, *outof),
        3_000_000_000,
        [pltpu.VMEM((2, SIDE, 2 * D), F32)],
    )
    kv_edge, placed = held(kv_edge), held(placed)
    (near,) = call(
        near_kernel,
        "near",
        [((2, EDGE, D), F32)],
        (pay1, pay2, far1, far2, over2, qlab, qkv, kv_edge, *norm, *into),
        1_000_000_000,
    )
    near = held(near)
    bend, other = call(third_kernel, "third", [((EDGE + 8, D), BF16)] * 2, (over1, kv_edge), 1_000_000)
    bend3 = swap_corners(bend, "lon")
    bend4 = swap(other, "lon", 0)
    (out,) = call(
        outer_kernel,
        "outer",
        [((2 * SIDE, D), BF16)],
        (
            *(pay1, pay2, far1, far2, over1, bend1, bend2, bend3, bend4, near),
            *(qlab, qkv, kv_edge, placed, back_edge, *norm, *into, *outof),
        ),
        1_500_000_000,
        [pltpu.VMEM((2, SIDE, D), BF16), pltpu.SemaphoreType.DMA((4,))],
        keep=False,
    )
    return out.reshape(LEV, COLS, ROWS, D).transpose(0, 2, 1, 3)


def solution(mesh):
    return jax.shard_map(
        local,
        mesh=mesh,
        in_specs=(P(None, "lat", "lon", None), P(None, "lat", "lon"), P(), P(), P(), P(), P(), P()),
        out_specs=P(None, "lat", "lon", None),
        check_vma=False,
    )
```
